256 devices in a mesh: row: 4 (over x), col: 8 (over z_lo, core), depth: 8 (over y, z_hi).
Axes of the slice: x: 4, y: 4, z: 8 (z_hi: 2, z_lo: 4; z = z_hi * 4 + z_lo), core: 2. Of those that a mesh axis runs over, the one named last changes fastest.
Arguments:
- factors: bfloat16 [1280, 480, 480], P(('row', 'col', 'depth')), may hold values from -0.15625 to 0.15625
- amplitudes: bfloat16 [528, 3, 480], P('row', None, 'depth'), may hold values from -0.15625 to 0.15625
Outputs:
- ladder: bfloat16 [528, 480, 480], P('row', 'depth', 'col')
The draws below stay inside these ranges and needn't reach their ends.
All inputs are finite; a program needn't handle non-finite values.
Results may differ from the reference program's by a relative error of at most 0.015.
Values may be sent and summed in bfloat16 or wider, within the bound.
A program may use at most 192 MiB of HBM per device.

```python
import jax
import jax.numpy as jnp
from jax import lax

NV = 480
NAUX = 1280
CW = 3
PAIRS = 528
D_BLOCK = 60
N_DEPTH = 8


def block_levels(rng, shape, split, smallest, top_value):
    level, own = 1.0, jax.random.fold_in(rng, 6)
    for position, shards_of in split:
        steps = jnp.exp(jax.random.uniform(jax.random.fold_in(own, position), (shards_of,), jnp.float32, smallest / len(split), top_value / len(split)))
        level = level * jnp.repeat(steps, shape[position] // shards_of).reshape([-1 if axis == position else 1 for axis in range(len(shape))])
    return level


def centred(own_key, shape, deviation, bound, pieces=(), dtype=jnp.bfloat16):
    drawn = jax.random.normal(own_key, shape, jnp.float32) * deviation
    if len(pieces) > 0:
        drawn = block_levels(own_key, shape, pieces, -0.22, 0.18) * drawn
    return jnp.clip(drawn, min=-bound, max=bound).astype(dtype)


def setup_inputs(seed: int = 0) -> dict:
    seeds = jax.random.split(jax.random.key(seed), 3)
    return {
        "factors": centred(seeds[0], (NAUX, NV, NV), NAUX ** -0.5, 0.15625, ((0, 256),)),
        "amplitudes": centred(seeds[1], (PAIRS, CW, NV), (CW * NV) ** -0.5, 0.15625, ((0, 4), (2, 8))),
    }


def reference(factors, amplitudes):
    left_side = factors[:, :, :CW]
    right_blocks = factors.reshape(NAUX, NV, N_DEPTH, D_BLOCK).transpose(2, 0, 1, 3)
    amp_blocks = amplitudes.reshape(PAIRS, CW, N_DEPTH, D_BLOCK).transpose(2, 0, 1, 3)

    def add_block(summed, inputs):
        right_block, amp_block = inputs
        rebuilt = lax.dot_general(left_side, right_block, (((0,), (0,)), ((), ())), preferred_element_type=jnp.float32)
        rebuilt = lax.optimization_barrier(rebuilt.astype(jnp.bfloat16)).astype(jnp.float32)
        partial_sum = jnp.einsum("acbd,pcd->pab", rebuilt, amp_block.astype(jnp.float32))
        partial_sum = lax.optimization_barrier(partial_sum.astype(jnp.bfloat16)).astype(jnp.float32)
        return summed + partial_sum, None

    start = jnp.zeros((PAIRS, NV, NV), jnp.float32)
    summed, _ = lax.scan(add_block, start, (right_blocks, amp_blocks))
    return summed.astype(jnp.bfloat16)
```

```python
import jax
import jax.numpy as jnp
from jax import lax
from jax.experimental import pallas as pl
from jax.experimental.pallas import tpu as pltpu
from jax.sharding import PartitionSpec as P

NV = 480
BLOCKS = 8
BLOCK = 60
PAD = 64
NVP = BLOCKS * PAD
LANE = 128
TILES = NVP // LANE
Q_LOCAL = 5
DEVICES = 256
NAUX = Q_LOCAL * DEVICES
CW = 3
ROWS_X = 132
GROUPS = 17
ROWS_P = GROUPS * 8
PAIR_ROWS = 4 * ROWS_P
B_PAIRS = 240
ACTIVE = 30
KDIM = CW * NVP
BF16 = jnp.bfloat16
F32 = jnp.float32
MIB = 1 << 20


def ones_where(mask):
    return jnp.where(mask, 1.0, 0.0).astype(BF16)


def iotas(rows, columns):
    shape = (rows, columns)
    return lax.broadcasted_iota(jnp.int32, shape, 0), lax.broadcasted_iota(jnp.int32, shape, 1)


def dot(left, right):
    return jnp.dot(left, right, preferred_element_type=F32)


def dot_nt(left, right):
    return lax.dot_general(left, right, (((1,), (1,)), ((), ())), preferred_element_type=F32)


def spread_matrix():
    row, column = iotas(NV, NVP)
    within = column & (PAD - 1)
    return ones_where((row == (column >> 6) * BLOCK + within) & (within < BLOCK))


def prep_kernel(f_ref, t_ref, send_ref, left_ref, t_out_ref):
    spread = spread_matrix()
    out_row, in_row = iotas(LANE, LANE)
    gather_rows = ones_where(
        in_row == (out_row & 3) * 32 + (out_row >> 3) * 2 + ((out_row >> 2) & 1)
    )
    row, column = iotas(16, NV)
    pick = ones_where((row == column) & (row < CW))
    left_tiles = []
    for q in range(Q_LOCAL):
        wide = dot(f_ref[q], spread).astype(BF16)
        for chunk in range(NV // 32):
            rows = wide[32 * chunk : 32 * chunk + 32]
            stacked = jnp.concatenate(
                [rows[:, LANE * t : LANE * (t + 1)] for t in range(TILES)], axis=0
            )
            moved = dot(gather_rows, stacked).reshape(16, 8, LANE)
            send_ref[16 * chunk : 16 * chunk + 16, q] = moved.astype(BF16)
        picked = dot(dot_nt(pick, f_ref[q]).astype(BF16), spread).astype(BF16)
        left_tiles += [picked[:, LANE * t : LANE * (t + 1)] for t in range(TILES)]
    out_row, in_row = iotas(64, 64 * Q_LOCAL)
    place = ones_where(
        (out_row == (in_row >> 6) * 12 + (in_row & 15) * 4 + ((in_row >> 4) & 3))
        & ((in_row & 15) < CW)
    )
    left_ref[...] = dot(place, jnp.concatenate(left_tiles, axis=0)).reshape(8, 8, LANE).astype(BF16)
    z_hi = lax.rem(lax.axis_index("depth"), 2)
    row, column = iotas(BLOCK, LANE)
    low = ones_where(row == column)
    high = ones_where(row + PAD == column)
    either = ones_where(row + PAD * z_hi == column)
    t_out_ref[0] = (dot(t_ref[0], low) + dot(t_ref[1], high)).astype(BF16)
    t_out_ref[1] = dot(t_ref[2], either).astype(BF16)


def place_of(row, col, depth):
    return row, depth // 2, (depth % 2) * 4 + col // 2, col % 2


def mesh_id(x, y, z, core):
    return {"row": x, "col": (z % 4) * 2 + core, "depth": y * 2 + z // 4}


def exchange_kernel(
    send_ref, left_in, t_in, right_ref, left_ref, t_ref,
    a2a_send, a2a_recv, l_send, l_recv, t_send, t_recv, own_sem,
):
    x, y, z, core = place_of(lax.axis_index("row"), lax.axis_index("col"), lax.axis_index("depth"))
    z_hi = z // 4
    me = core * 128 + x * 32 + y * 8 + z
    active = x * 8 + y * 2 + z_hi < ACTIVE

    def remote(src, dst, send, recv, to):
        return pltpu.make_async_remote_copy(
            src_ref=src, dst_ref=dst, send_sem=send, recv_sem=recv,
            device_id=mesh_id(*to), device_id_type=pl.DeviceIdType.MESH,
        )

    def wait(ref, sem):
        pltpu.make_async_copy(ref, ref, sem).wait()

    own_left = pltpu.make_async_copy(left_in, left_ref.at[:, core, x, y, z], own_sem.at[0])
    own_left.start()
    own_t = pltpu.make_async_copy(t_in.at[core], t_ref.at[core, x, y, z_hi], own_sem.at[1])
    own_t.start()
    remote(
        t_in.at[core], t_ref.at[core, x, y, z_hi], t_send.at[0], t_recv.at[0], (x, y, 7 - z, core)
    ).start()

    @pl.loop(1, 8)
    def _(step):
        remote(
            left_in, left_ref.at[:, core, x, y, z], l_send.at[0], l_recv.at[0],
            (x, y, (z + step) % 8, core),
        ).start()

    def send_right(first, last):
        @pl.loop(first, last)
        def _(step):
            to_z = (z + step) % 8
            to_core = (core + step // 8) % 2
            to_y = (y + step // 16) % 4
            to_x = (x + step // 64) % 4
            group = to_x * 8 + to_y * 2 + to_z // 4
            pair = ACTIVE * (((to_z + 2) % 4) * 2 + to_core) + group

            @pl.when(group < ACTIVE)
            def _():
                remote(
                    send_ref.at[pair], right_ref.at[:, me], a2a_send, a2a_recv,
                    (to_x, to_y, to_z, to_core),
                ).start()

    @pl.when(active)
    def _():
        pair = ACTIVE * (((z + 2) % 4) * 2 + core) + x * 8 + y * 2 + z_hi
        pltpu.make_async_copy(send_ref.at[pair], right_ref.at[:, me], own_sem.at[2]).start()

    send_right(1, 64)

    own_left.wait()
    wait(left_ref.at[:, 0, 0, 0, 0:7], l_recv.at[0])
    own_t.wait()
    wait(t_ref.at[0, 0, 0, 0], t_recv.at[0])

    @pl.loop(1, 4)
    def _(step):
        block = left_ref.at[0:4, core, x, y]
        remote(block, block, l_send.at[1], l_recv.at[1], (x, (y + step) % 4, z, core)).start()
        block = left_ref.at[4:8, core, x, y]
        remote(block, block, l_send.at[2], l_recv.at[2], ((x + step) % 4, y, z, core)).start()
        block = t_ref.at[core, x, y]
        to = ((x + step * core) % 4, (y + step * (1 - core)) % 4, z, core)
        remote(block, block, t_send.at[1], t_recv.at[1], to).start()

    send_right(64, 128)

    wait(left_ref.at[0:4, 0, 0, 0:3], l_recv.at[1])
    wait(left_ref.at[0:4, 0, 0, 0:3], l_recv.at[2])
    wait(t_ref.at[0, 0, 0:3], t_recv.at[1])

    @pl.loop(1, 4)
    def _(step):
        block = left_ref.at[0:4, core, x]
        remote(block, block, l_send.at[3], l_recv.at[3], ((x + step) % 4, y, z, core)).start()
        block = left_ref.at[4:8, core, :, y]
        remote(block, block, l_send.at[4], l_recv.at[4], (x, (y + step) % 4, z, core)).start()

        @pl.when(core == 0)
        def _():
            block = t_ref.at[0, x]
            remote(block, block, t_send.at[2], t_recv.at[2], ((x + step) % 4, y, z, core)).start()

        @pl.when(core == 1)
        def _():
            block = t_ref.at[1, :, y]
            remote(block, block, t_send.at[2], t_recv.at[2], (x, (y + step) % 4, z, core)).start()

    send_right(128, 256)

    wait(left_ref.at[0:4, 0, 0:3], l_recv.at[3])
    wait(left_ref.at[0:4, 0, 0:3], l_recv.at[4])
    sibling = (x, y, z, 1 - core)
    block = left_ref.at[:, core]
    swap_left = remote(block, block, l_send.at[5], l_recv.at[5], sibling)
    swap_left.start()
    wait(t_ref.at[0, 0:3], t_recv.at[2])
    block = t_ref.at[core]
    swap_t = remote(block, block, t_send.at[3], t_recv.at[3], sibling)
    swap_t.start()

    swap_left.wait()
    swap_t.wait()
    wait(left_ref.at[:, 0, 0, 0, 0:7], l_send.at[0])
    wait(left_ref.at[0:4, 0, 0, 0:3], l_send.at[1])
    wait(left_ref.at[0:4, 0, 0, 0:3], l_send.at[2])
    wait(left_ref.at[0:4, 0, 0:3], l_send.at[3])
    wait(left_ref.at[0:4, 0, 0:3], l_send.at[4])
    wait(t_ref.at[0, 0, 0, 0], t_send.at[0])
    wait(t_ref.at[0, 0, 0:3], t_send.at[1])
    wait(t_ref.at[0, 0:3], t_send.at[2])

    @pl.when(active)
    def _():
        wait(send_ref.at[0 : B_PAIRS - 1], a2a_send)
        wait(right_ref.at[:, 0], own_sem.at[2])
        wait(right_ref.at[:, 0 : DEVICES - 1], a2a_recv)

    @pl.when(jnp.logical_not(active))
    def _():
        wait(send_ref, a2a_send)


def compute_kernel(right_ref, left_ref, t_ref, out_ref, left2, right_n, right_t, mid, t_cat, total):
    out_row, in_row = iotas(256, 256)
    sort_rows = ones_where(in_row == ((out_row & 31) << 3) + (out_row >> 5))
    row, column = iotas(LANE, LANE)
    identity = ones_where(row == column)

    for q in range(Q_LOCAL):
        for chunk in range(8):
            block = right_ref[q, 32 * chunk : 32 * chunk + 32].astype(F32).reshape(256, LANE)
            moved = dot(sort_rows, block.astype(BF16)).astype(BF16)
            for r in range(8):
                base = 256 * q + 32 * chunk
                right_n[r, base : base + 32, :] = moved[32 * r : 32 * r + 32]
        for r in range(8):
            block = right_n[r, 256 * q : 256 * q + 256, :]
            right_t[LANE * r : LANE * r + LANE, 256 * q : 256 * q + 256] = dot_nt(
                identity, block
            ).astype(BF16)
    for group in range(8):
        for chunk in range(8):
            block = left_ref[group, 32 * chunk : 32 * chunk + 32].astype(F32).reshape(256, LANE)
            moved = dot(sort_rows, block.astype(BF16)).astype(BF16)
            for r in range(8):
                q, tile = divmod(8 * group + r, 12)
                if q < Q_LOCAL:
                    base = 256 * q + 32 * chunk
                    left2[base : base + 32, LANE * tile : LANE * tile + LANE] = moved[
                        32 * r : 32 * r + 32
                    ]
    for m in range(4):
        which, half = divmod(m, 2)
        for c in range(CW):
            rebuilt = dot(
                right_t[256 * m : 256 * m + 256, :], left2[:, NVP * c : NVP * c + NVP]
            ).astype(BF16)
            if c < 2:
                for k in range(4):
                    base = (4 * half + k) * LANE + PAD * c
                    mid[which, base : base + PAD, :] = rebuilt[PAD * k : PAD * k + PAD]
            else:
                base = 2 * NVP + 256 * half
                mid[which, base : base + 256, :] = rebuilt
    for x in range(4):
        rows = slice(ROWS_P * x, ROWS_P * x + ROWS_P)
        for k in range(BLOCKS):
            t_cat[rows, LANE * k : LANE * k + LANE] = t_ref[0, x, k].astype(F32)
        for y in range(4):
            base = 2 * NVP + LANE * y
            t_cat[rows, base : base + LANE] = t_ref[1, x, 2 * y].astype(F32) + t_ref[
                1, x, 2 * y + 1
            ].astype(F32)
    t_all = t_cat[...].astype(BF16)
    for which in range(2):
        total[which] = dot(t_all, mid[which])
    first_half = lax.broadcasted_iota(jnp.int32, (ROWS_P, LANE), 1) < PAD
    for x in range(4):
        rows = slice(ROWS_P * x, ROWS_P * x + ROWS_P)
        for y in range(4):
            lanes = slice(LANE * y, LANE * y + LANE)
            one, two = total[0, rows, lanes], total[1, rows, lanes]
            even = jnp.where(first_half, one, pltpu.roll(two, PAD, 1))
            odd = jnp.where(first_half, pltpu.roll(one, PAD, 1), two)
            out_ref[x, 2 * y] = even.reshape(GROUPS, 8, LANE).astype(BF16)
            out_ref[x, 2 * y + 1] = odd.reshape(GROUPS, 8, LANE).astype(BF16)


def scatter_kernel(in_ref, out_ref, send_sem, recv_sem):
    x, y, z, core = place_of(lax.axis_index("row"), lax.axis_index("col"), lax.axis_index("depth"))
    group = x * 8 + y * 2 + z // 4

    @pl.when(group < ACTIVE)
    def _():
        @pl.loop(0, 32)
        def _(step):
            to_z = (z + 2 + 4 * (step % 2)) % 8
            to_y = (y + step // 2) % 4
            to_x = (x + step // 8) % 4
            pltpu.make_async_remote_copy(
                src_ref=in_ref.at[to_x, to_y * 2 + to_z // 4],
                dst_ref=out_ref.at[group],
                send_sem=send_sem,
                recv_sem=recv_sem,
                device_id=mesh_id(to_x, to_y, to_z, core),
                device_id_type=pl.DeviceIdType.MESH,
            ).start()

    block = out_ref.at[0:ACTIVE]
    pltpu.make_async_copy(block, block, recv_sem).wait()

    @pl.when(group < ACTIVE)
    def _():
        pltpu.make_async_copy(in_ref, in_ref, send_sem).wait()


def finish_kernel(in_ref, out_ref, turned, result):
    row, column = iotas(LANE, LANE)
    identity = ones_where(row == column)
    row, column = iotas(512, 1024)
    place = ones_where(
        ((column >> 7) == (row & 7)) & ((column & 127) == 2 * ((row >> 3) & 31) + (row >> 8))
    )
    for group in range(GROUPS):
        block = in_ref[0:ACTIVE, group].astype(F32).reshape(8 * ACTIVE, LANE)
        block = jnp.concatenate([block, jnp.zeros((16, LANE), F32)], axis=0).astype(BF16)
        flipped = dot_nt(identity, block).astype(BF16)
        turned[PAD * group : PAD * group + PAD, 0:256] = flipped[0:PAD]
        turned[PAD * group : PAD * group + PAD, 256:512] = flipped[PAD:LANE]
    result[...] = dot(turned[...], place)
    for pair in range(ROWS_X):
        group, within = divmod(pair, 8)
        block = result[PAD * group : PAD * group + PAD, LANE * within : LANE * within + LANE]
        out_ref[pair] = block.astype(BF16)[0:BLOCK, 0:BLOCK]


def vmem(count):
    return [pl.BlockSpec(memory_space=pltpu.VMEM)] * count


def anywhere(count):
    return [pl.BlockSpec(memory_space=pl.ANY)] * count


def shape(*sizes):
    return jax.ShapeDtypeStruct(sizes, BF16)


def prepare(factors, amplitudes):
    t_local = jnp.pad(amplitudes.transpose(1, 0, 2), ((0, 0), (0, ROWS_P - ROWS_X), (0, 0)))
    return pl.pallas_call(
        prep_kernel,
        out_shape=(shape(B_PAIRS, Q_LOCAL, 8, LANE), shape(8, 8, LANE), shape(2, ROWS_P, LANE)),
        in_specs=vmem(2),
        out_specs=tuple(vmem(3)),
        compiler_params=pltpu.CompilerParams(vmem_limit_bytes=40 * MIB),
        name="prepare",
    )(factors, t_local)


def exchange(send, left_own, t_own):
    dma = pltpu.SemaphoreType.DMA
    return pl.pallas_call(
        exchange_kernel,
        out_shape=(
            shape(Q_LOCAL, DEVICES, 8, LANE),
            shape(8, 2, 4, 4, 8, 8, LANE),
            shape(2, 4, 4, 2, ROWS_P, LANE),
        ),
        in_specs=anywhere(3),
        out_specs=tuple(anywhere(3)),
        scratch_shapes=[dma, dma, dma((6,)), dma((6,)), dma((4,)), dma((4,)), dma((3,))],
        compiler_params=pltpu.CompilerParams(has_side_effects=True),
        name="exchange",
    )(send, left_own, t_own)


def compute(right, left, t_full):
    return pl.pallas_call(
        compute_kernel,
        out_shape=shape(4, BLOCKS, GROUPS, 8, LANE),
        in_specs=vmem(3),
        out_specs=vmem(1)[0],
        scratch_shapes=[
            pltpu.VMEM((NAUX, KDIM), BF16),
            pltpu.VMEM((8, NAUX, LANE), BF16),
            pltpu.VMEM((2 * NVP, NAUX), BF16),
            pltpu.VMEM((2, KDIM, NVP), BF16),
            pltpu.VMEM((PAIR_ROWS, KDIM), F32),
            pltpu.VMEM((2, PAIR_ROWS, NVP), F32),
        ],
        compiler_params=pltpu.CompilerParams(vmem_limit_bytes=56 * MIB),
        name="compute",
    )(
        right,
        left.reshape(8, DEVICES, 8, LANE),
        t_full.reshape(2, 4, BLOCKS, ROWS_P, LANE),
    )


def scatter(blocks):
    dma = pltpu.SemaphoreType.DMA
    return pl.pallas_call(
        scatter_kernel,
        out_shape=shape(32, GROUPS, 8, LANE),
        in_specs=anywhere(1),
        out_specs=anywhere(1)[0],
        scratch_shapes=[dma, dma],
        compiler_params=pltpu.CompilerParams(has_side_effects=True),
        name="scatter",
    )(blocks)


def finish(blocks):
    return pl.pallas_call(
        finish_kernel,
        out_shape=shape(ROWS_X, BLOCK, BLOCK),
        in_specs=vmem(1),
        out_specs=vmem(1)[0],
        scratch_shapes=[
            pltpu.VMEM((PAD * GROUPS, 512), BF16),
            pltpu.VMEM((PAD * GROUPS, 1024), F32),
        ],
        compiler_params=pltpu.CompilerParams(vmem_limit_bytes=40 * MIB),
        name="finish",
    )(blocks)


def on_device(factors, amplitudes):
    return finish(scatter(compute(*exchange(*prepare(factors, amplitudes)))))


def solution(mesh):
    in_specs = (P(("row", "col", "depth"), None, None), P("row", None, "depth"))
    out_specs = P("row", "depth", "col")
    return jax.shard_map(
        on_device, mesh=mesh, in_specs=in_specs, out_specs=out_specs, check_vma=False
    )
```

```python
import jax
import jax.numpy as jnp
from jax import lax
from jax.experimental import pallas as pl
from jax.experimental.pallas import tpu as pltpu
from jax.sharding import PartitionSpec as P

NV = 480
BLOCKS = 8
BLOCK = 60
PAD = 64
NVP = BLOCKS * PAD
LANE = 128
TILES = NVP // LANE
Q_LOCAL = 5
DEVICES = 256
NAUX = Q_LOCAL * DEVICES
CW = 3
ROWS_X = 132
GROUPS = 17
ROWS_P = GROUPS * 8
B_PAIRS = 240
ACTIVE = 30
KDIM = CW * NVP
LEFT_ROWS = Q_LOCAL * CW * TILES
BF16 = jnp.bfloat16
F32 = jnp.float32
MIB = 1 << 20


def ones_where(mask):
    return jnp.where(mask, 1.0, 0.0).astype(BF16)


def iotas(rows, columns):
    shape = (rows, columns)
    return lax.broadcasted_iota(jnp.int32, shape, 0), lax.broadcasted_iota(jnp.int32, shape, 1)


def dot(left, right):
    return jnp.dot(left, right, preferred_element_type=F32)


def dot_nt(left, right):
    return lax.dot_general(left, right, (((1,), (1,)), ((), ())), preferred_element_type=F32)


def spread_matrix():
    row, column = iotas(NV, NVP)
    within = column & (PAD - 1)
    return ones_where((row == (column >> 6) * BLOCK + within) & (within < BLOCK))


def prep_kernel(f_ref, t_ref, send_ref, left_ref, t_out_ref):
    spread = spread_matrix()
    out_row, in_row = iotas(LANE, LANE)
    gather_rows = ones_where(
        in_row == (out_row & 3) * 32 + (out_row >> 3) * 2 + ((out_row >> 2) & 1)
    )
    row, column = iotas(16, NV)
    pick = ones_where((row == column) & (row < CW))
    left_tiles = []
    for q in range(Q_LOCAL):
        wide = dot(f_ref[q], spread).astype(BF16)
        for chunk in range(NV // 32):
            rows = wide[32 * chunk : 32 * chunk + 32]
            stacked = jnp.concatenate(
                [rows[:, LANE * t : LANE * (t + 1)] for t in range(TILES)], axis=0
            )
            moved = dot(gather_rows, stacked).reshape(16, 8, LANE)
            send_ref[16 * chunk : 16 * chunk + 16, q] = moved.astype(BF16)
        picked = dot(dot_nt(pick, f_ref[q]).astype(BF16), spread).astype(BF16)
        left_tiles += [picked[:, LANE * t : LANE * (t + 1)] for t in range(TILES)]
    out_row, in_row = iotas(64, 64 * Q_LOCAL)
    place = ones_where(
        (out_row == (in_row >> 6) * 12 + (in_row & 15) * 4 + ((in_row >> 4) & 3))
        & ((in_row & 15) < CW)
    )
    left_ref[...] = dot(place, jnp.concatenate(left_tiles, axis=0)).reshape(8, 8, LANE).astype(BF16)
    z_hi = lax.rem(lax.axis_index("depth"), 2)
    row, column = iotas(BLOCK, LANE)
    low = ones_where(row == column)
    high = ones_where(row + PAD == column)
    either = ones_where(row + PAD * z_hi == column)
    both = dot(t_ref[0], low) + dot(t_ref[1], high)
    t_out_ref[0] = both.reshape(GROUPS, 8, LANE).astype(BF16)
    t_out_ref[1] = dot(t_ref[2], either).reshape(GROUPS, 8, LANE).astype(BF16)


def place_of(row, col, depth):
    return row, depth // 2, (depth % 2) * 4 + col // 2, col % 2


def mesh_id(x, y, z, core):
    return {"row": x, "col": (z % 4) * 2 + core, "depth": y * 2 + z // 4}


def wait_bytes(ref, sem):
    pltpu.make_async_copy(ref, ref, sem).wait()


def exchange_kernel(
    send_ref, left_in, t_in, right_ref, left_ref, t_ref,
    staged, bundle, a2a_send, a2a_recv, l_send, l_recv, t_send, t_recv, own_sem,
):
    x, y, z, core = place_of(lax.axis_index("row"), lax.axis_index("col"), lax.axis_index("depth"))
    z_hi = z // 4
    me = core * 128 + x * 32 + y * 8 + z
    active = x * 8 + y * 2 + z_hi < ACTIVE
    half = LEFT_ROWS // 2

    def remote(src, dst, send, recv, to):
        return pltpu.make_async_remote_copy(
            src_ref=src, dst_ref=dst, send_sem=send, recv_sem=recv,
            device_id=mesh_id(*to), device_id_type=pl.DeviceIdType.MESH,
        )

    own_left = pltpu.make_async_copy(left_in, staged.at[z], own_sem.at[0])
    own_left.start()
    own_t = pltpu.make_async_copy(t_in.at[core], t_ref.at[core, y, z_hi, x], own_sem.at[1])
    own_t.start()
    remote(
        t_in.at[core], t_ref.at[core, y, z_hi, x], t_send.at[0], t_recv.at[0], (x, y, 7 - z, core)
    ).start()

    @pl.loop(1, 8)
    def _(step):
        remote(
            left_in, staged.at[z], l_send.at[0], l_recv.at[0], (x, y, (z + step) % 8, core)
        ).start()

    def send_right(first, last):
        @pl.loop(first, last)
        def _(step):
            to_z = (z + step) % 8
            to_core = (core + step // 8) % 2
            to_y = (y + step // 16) % 4
            to_x = (x + step // 64) % 4
            group = to_x * 8 + to_y * 2 + to_z // 4
            pair = ACTIVE * (((to_z + 2) % 4) * 2 + to_core) + group

            @pl.when(group < ACTIVE)
            def _():
                remote(
                    send_ref.at[pair], right_ref.at[:, me], a2a_send, a2a_recv,
                    (to_x, to_y, to_z, to_core),
                ).start()

    @pl.when(active)
    def _():
        pair = ACTIVE * (((z + 2) % 4) * 2 + core) + x * 8 + y * 2 + z_hi
        pltpu.make_async_copy(send_ref.at[pair], right_ref.at[:, me], own_sem.at[2]).start()

    send_right(1, 16)

    own_left.wait()
    wait_bytes(staged.at[0:7], l_recv.at[0])
    out_row, in_row = iotas(64, 64)
    sort_rows = ones_where(in_row == ((out_row & 7) << 3) + (out_row >> 3))
    wide = jnp.concatenate(
        [staged[:, g].astype(F32).reshape(64, LANE) for g in range(8)], axis=1
    ).astype(BF16)
    wide = dot(sort_rows, wide)
    for g in range(8):
        block = wide[:, LANE * g : LANE * g + LANE].reshape(8, 8, LANE).astype(BF16)
        bundle[8 * g : 8 * g + 8] = block
    own_bundle = pltpu.make_async_copy(
        bundle.at[0:LEFT_ROWS], left_ref.at[:, core, x, y], own_sem.at[0]
    )
    own_bundle.start()
    own_t.wait()
    wait_bytes(t_ref.at[0, 0, 0, 0], t_recv.at[0])

    @pl.loop(1, 4)
    def _(step):
        remote(
            bundle.at[0:half], left_ref.at[0:half, core, x, y], l_send.at[1], l_recv.at[1],
            (x, (y + step) % 4, z, core),
        ).start()
        remote(
            bundle.at[half:LEFT_ROWS], left_ref.at[half:LEFT_ROWS, core, x, y],
            l_send.at[2], l_recv.at[2], ((x + step) % 4, y, z, core),
        ).start()
        block = t_ref.at[core, y, :, x]
        to = ((x + step * core) % 4, (y + step * (1 - core)) % 4, z, core)
        remote(block, block, t_send.at[1], t_recv.at[1], to).start()

    send_right(16, 48)

    own_bundle.wait()
    three_bundles = left_ref.at[0:half, 0, 0, 0:3]
    three_rings = left_ref.at[0:half, 0, 0:3]
    wait_bytes(three_bundles, l_recv.at[1])
    wait_bytes(three_bundles, l_recv.at[2])
    wait_bytes(t_ref.at[0, 0, :, 0:3], t_recv.at[1])

    @pl.loop(1, 4)
    def _(step):
        block = left_ref.at[0:half, core, x]
        remote(block, block, l_send.at[3], l_recv.at[3], ((x + step) % 4, y, z, core)).start()
        block = left_ref.at[half:LEFT_ROWS, core, :, y]
        remote(block, block, l_send.at[4], l_recv.at[4], (x, (y + step) % 4, z, core)).start()

        @pl.when(core == 0)
        def _():
            block = t_ref.at[0, :, :, x]
            remote(block, block, t_send.at[2], t_recv.at[2], ((x + step) % 4, y, z, core)).start()

        @pl.when(core == 1)
        def _():
            block = t_ref.at[1, y]
            remote(block, block, t_send.at[2], t_recv.at[2], (x, (y + step) % 4, z, core)).start()

    send_right(48, 128)

    wait_bytes(three_rings, l_recv.at[3])
    wait_bytes(three_rings, l_recv.at[4])
    sibling = (x, y, z, 1 - core)
    block = left_ref.at[:, core]
    swap_left = remote(block, block, l_send.at[5], l_recv.at[5], sibling)
    swap_left.start()
    wait_bytes(t_ref.at[0, 0:3], t_recv.at[2])
    block = t_ref.at[core]
    swap_t = remote(block, block, t_send.at[3], t_recv.at[3], sibling)
    swap_t.start()

    send_right(128, 256)

    swap_left.wait()
    swap_t.wait()
    wait_bytes(staged.at[0:7], l_send.at[0])
    wait_bytes(three_bundles, l_send.at[1])
    wait_bytes(three_bundles, l_send.at[2])
    wait_bytes(three_rings, l_send.at[3])
    wait_bytes(three_rings, l_send.at[4])
    wait_bytes(t_ref.at[0, 0, 0, 0], t_send.at[0])
    wait_bytes(t_ref.at[0, 0, :, 0:3], t_send.at[1])
    wait_bytes(t_ref.at[0, 0:3], t_send.at[2])

    @pl.when(active)
    def _():
        wait_bytes(send_ref.at[0 : B_PAIRS - 1], a2a_send)
        wait_bytes(right_ref.at[:, 0], own_sem.at[2])
        wait_bytes(right_ref.at[:, 0 : DEVICES - 1], a2a_recv)

    @pl.when(jnp.logical_not(active))
    def _():
        wait_bytes(send_ref, a2a_send)


def compute_kernel(
    right_ref, left_ref, t_ref, out_ref, right_n, right_t, mid, blocks, send_sem, recv_sem
):
    x, y, z, core = place_of(lax.axis_index("row"), lax.axis_index("col"), lax.axis_index("depth"))
    group = x * 8 + y * 2 + z // 4
    barrier = pltpu.get_barrier_semaphore()

    def partner(step):
        return (x + step // 8) % 4, (y + step // 2) % 4, (z + 2 + 4 * (step % 2)) % 8

    @pl.loop(0, 32)
    def _(step):
        pl.semaphore_signal(
            barrier, inc=1, device_id=mesh_id(*partner(step), core),
            device_id_type=pl.DeviceIdType.MESH,
        )

    @pl.when(group < ACTIVE)
    def _():
        out_row, in_row = iotas(256, 256)
        sort_rows = ones_where(in_row == ((out_row & 31) << 3) + (out_row >> 5))
        row, column = iotas(LANE, LANE)
        identity = ones_where(row == column)
        for q in range(Q_LOCAL):
            for chunk in range(0, 8, 2):
                block = jnp.concatenate(
                    [
                        right_ref[q, 32 * c : 32 * c + 32].astype(F32).reshape(256, LANE)
                        for c in (chunk, chunk + 1)
                    ],
                    axis=1,
                )
                moved = dot(sort_rows, block.astype(BF16)).astype(BF16)
                for r in range(8):
                    for c in range(2):
                        base = 256 * q + 32 * (chunk + c)
                        right_n[r, base : base + 32, :] = moved[
                            32 * r : 32 * r + 32, LANE * c : LANE * c + LANE
                        ]
            for r in range(8):
                block = right_n[r, 256 * q : 256 * q + 256, :]
                right_t[LANE * r : LANE * r + LANE, 256 * q : 256 * q + 256] = dot_nt(
                    identity, block
                ).astype(BF16)
        for c in range(CW):
            left = jnp.concatenate(
                [
                    jnp.concatenate(
                        [
                            left_ref[12 * q + 4 * c + t].reshape(256, LANE)
                            for t in range(TILES)
                        ],
                        axis=1,
                    )
                    for q in range(Q_LOCAL)
                ],
                axis=0,
            )
            for m in range(4):
                which, half = divmod(m, 2)
                rebuilt = dot(right_t[256 * m : 256 * m + 256, :], left).astype(BF16)
                if c < 2:
                    for k in range(4):
                        base = (4 * half + k) * LANE + PAD * c
                        mid[which, base : base + PAD, :] = rebuilt[PAD * k : PAD * k + PAD]
                else:
                    base = 2 * NVP + 256 * half
                    mid[which, base : base + 256, :] = rebuilt

    pl.semaphore_wait(barrier, 32)

    @pl.when(group < ACTIVE)
    def _():
        first_half = lax.broadcasted_iota(jnp.int32, (ROWS_P, LANE), 1) < PAD

        @pl.loop(0, 4)
        def _(turn):
            to_x = (x + turn) % 4

            def tile(kind, k):
                return t_ref[kind, k // 2, k % 2, to_x].astype(F32).reshape(ROWS_P, LANE)

            tiles = [tile(0, k) for k in range(BLOCKS)]
            tiles += [tile(1, 2 * k) + tile(1, 2 * k + 1) for k in range(4)]
            t_rows = jnp.concatenate(tiles, axis=1).astype(BF16)
            totals = [dot(t_rows, mid[which]) for which in range(2)]
            for k in range(4):
                lanes = slice(LANE * k, LANE * k + LANE)
                one, two = totals[0][:, lanes], totals[1][:, lanes]
                even = jnp.where(first_half, one, pltpu.roll(two, PAD, 1))
                odd = jnp.where(first_half, pltpu.roll(one, PAD, 1), two)
                blocks[to_x, 2 * k] = even.reshape(GROUPS, 8, LANE).astype(BF16)
                blocks[to_x, 2 * k + 1] = odd.reshape(GROUPS, 8, LANE).astype(BF16)

            @pl.loop(0, 8)
            def _(step):
                _, to_y, to_z = partner(step)
                pltpu.make_async_remote_copy(
                    src_ref=blocks.at[to_x, to_y * 2 + to_z // 4],
                    dst_ref=out_ref.at[group],
                    send_sem=send_sem,
                    recv_sem=recv_sem,
                    device_id=mesh_id(to_x, to_y, to_z, core),
                    device_id_type=pl.DeviceIdType.MESH,
                ).start()

    wait_bytes(out_ref.at[0:ACTIVE], recv_sem)

    @pl.when(group < ACTIVE)
    def _():
        wait_bytes(blocks, send_sem)


def finish_kernel(in_ref, out_ref, turned):
    row, column = iotas(LANE, LANE)
    identity = ones_where(row == column)
    for group in range(ACTIVE):
        block = in_ref[group].astype(F32).reshape(ROWS_P, LANE).astype(BF16)
        turned[group] = dot_nt(identity, block)
    rows = 2 * ACTIVE * 8
    out_row, in_row = iotas(512, rows)
    sort_rows = ones_where(in_row == ((out_row & 63) << 3) + (out_row >> 6))
    for chunk in range(8):
        parts = []
        for group in range(ACTIVE):
            for which in range(2):
                base = PAD * which + 8 * chunk
                parts.append(turned[group, base : base + 8, :])
        moved = dot(sort_rows, jnp.concatenate(parts, axis=0).astype(BF16)).astype(BF16)
        for a in range(8 if chunk < 7 else 4):
            out_ref[8 * chunk + a] = moved[64 * a : 64 * a + 64][0:BLOCK, 0:ROWS_X]


def vmem(count):
    return [pl.BlockSpec(memory_space=pltpu.VMEM)] * count


def anywhere(count):
    return [pl.BlockSpec(memory_space=pl.ANY)] * count


def shape(*sizes):
    return jax.ShapeDtypeStruct(sizes, BF16)


def prepare(factors, amplitudes):
    t_local = jnp.pad(amplitudes.transpose(1, 0, 2), ((0, 0), (0, ROWS_P - ROWS_X), (0, 0)))
    return pl.pallas_call(
        prep_kernel,
        out_shape=(
            shape(B_PAIRS, Q_LOCAL, 8, LANE), shape(8, 8, LANE), shape(2, GROUPS, 8, LANE)
        ),
        in_specs=vmem(2),
        out_specs=tuple(vmem(3)),
        compiler_params=pltpu.CompilerParams(vmem_limit_bytes=40 * MIB),
        name="prepare",
    )(factors, t_local)


def exchange(send, left_own, t_own):
    dma = pltpu.SemaphoreType.DMA
    return pl.pallas_call(
        exchange_kernel,
        out_shape=(
            shape(Q_LOCAL, DEVICES, 8, LANE),
            shape(LEFT_ROWS, 2, 4, 4, 8, LANE),
            shape(2, 4, 2, 4, GROUPS, 8, LANE),
        ),
        in_specs=anywhere(3),
        out_specs=tuple(anywhere(3)),
        scratch_shapes=[
            pltpu.VMEM((8, 8, 8, LANE), BF16),
            pltpu.VMEM((64, 8, LANE), BF16),
            dma, dma, dma((6,)), dma((6,)), dma((4,)), dma((4,)), dma((3,)),
        ],
        compiler_params=pltpu.CompilerParams(has_side_effects=True, vmem_limit_bytes=4 * MIB),
        name="exchange",
    )(send, left_own, t_own)


def compute(right, left, t_full):
    dma = pltpu.SemaphoreType.DMA
    return pl.pallas_call(
        compute_kernel,
        out_shape=shape(32, GROUPS, 8, LANE),
        in_specs=vmem(3),
        out_specs=vmem(1)[0],
        scratch_shapes=[
            pltpu.VMEM((8, NAUX, LANE), BF16),
            pltpu.VMEM((2 * NVP, NAUX), BF16),
            pltpu.VMEM((2, KDIM, NVP), BF16),
            pltpu.VMEM((4, BLOCKS, GROUPS, 8, LANE), BF16),
            dma,
            dma,
        ],
        compiler_params=pltpu.CompilerParams(
            vmem_limit_bytes=28 * MIB, has_side_effects=True, collective_id=7
        ),
        name="compute",
    )(
        right,
        left.reshape(LEFT_ROWS, DEVICES // 8, 8, LANE),
        t_full,
    )


def finish(blocks):
    turned = pl.pallas_call(
        finish_kernel,
        out_shape=shape(BLOCK, BLOCK, ROWS_X),
        in_specs=vmem(1),
        out_specs=vmem(1)[0],
        scratch_shapes=[pltpu.VMEM((ACTIVE, LANE, ROWS_P), F32)],
        compiler_params=pltpu.CompilerParams(vmem_limit_bytes=40 * MIB),
        name="finish",
    )(blocks)
    return turned.transpose(2, 0, 1)


def on_device(factors, amplitudes):
    return finish(compute(*exchange(*prepare(factors, amplitudes))))


def solution(mesh):
    in_specs = (P(("row", "col", "depth"), None, None), P("row", None, "depth"))
    out_specs = P("row", "depth", "col")
    return jax.shard_map(
        on_device, mesh=mesh, in_specs=in_specs, out_specs=out_specs, check_vma=False
    )
```

```python
import jax
import jax.numpy as jnp
from jax import lax
from jax.experimental import pallas as pl
from jax.experimental.pallas import tpu as pltpu
from jax.sharding import PartitionSpec as P

NV = 480
BLOCKS = 8
BLOCK = 60
PAD = 64
NVP = BLOCKS * PAD
LANE = 128
TILES = NVP // LANE
Q_LOCAL = 5
DEVICES = 256
NAUX = Q_LOCAL * DEVICES
CW = 3
ROWS_X = 132
GROUPS = 17
ROWS_P = GROUPS * 8
B_PAIRS = 240
SLOTS = 15
ACTIVE = 2 * SLOTS
ORDER = ((2, 1), (1, 1), (3, 1), (0, 1), (2, 0), (1, 0), (3, 0), "beside", "own")
PARTS = len(ORDER)
KDIM = CW * NVP
LEFT_ROWS = Q_LOCAL * CW * TILES
BF16 = jnp.bfloat16
F32 = jnp.float32
MIB = 1 << 20


def ones_where(mask):
    return jnp.where(mask, 1.0, 0.0).astype(BF16)


def iotas(rows, columns):
    shape = (rows, columns)
    return lax.broadcasted_iota(jnp.int32, shape, 0), lax.broadcasted_iota(jnp.int32, shape, 1)


def dot(left, right):
    return jnp.dot(left, right, preferred_element_type=F32)


def dot_nt(left, right):
    return lax.dot_general(left, right, (((1,), (1,)), ((), ())), preferred_element_type=F32)


def spread_matrix():
    row, column = iotas(NV, NVP)
    within = column & (PAD - 1)
    return ones_where((row == (column >> 6) * BLOCK + within) & (within < BLOCK))


def prepare(f_ref, t_ref, send_ref, left_ref, t_out_ref):
    spread = spread_matrix()
    out_row, in_row = iotas(LANE, LANE)
    gather_rows = ones_where(
        in_row == (out_row & 3) * 32 + (out_row >> 3) * 2 + ((out_row >> 2) & 1)
    )
    row, column = iotas(16, NV)
    pick = ones_where((row == column) & (row < CW))
    left_tiles = []
    for q in range(Q_LOCAL):
        wide = dot(f_ref[q], spread).astype(BF16)
        for chunk in range(NV // 32):
            rows = wide[32 * chunk : 32 * chunk + 32]
            stacked = jnp.concatenate(
                [rows[:, LANE * t : LANE * (t + 1)] for t in range(TILES)], axis=0
            )
            moved = dot(gather_rows, stacked).reshape(16, 8, LANE)
            send_ref[16 * chunk : 16 * chunk + 16, q] = moved.astype(BF16)
        picked = dot(dot_nt(pick, f_ref[q]).astype(BF16), spread).astype(BF16)
        left_tiles += [picked[:, LANE * t : LANE * (t + 1)] for t in range(TILES)]
    out_row, in_row = iotas(64, 64 * Q_LOCAL)
    place = ones_where(
        (out_row == (in_row >> 6) * 12 + (in_row & 15) * 4 + ((in_row >> 4) & 3))
        & ((in_row & 15) < CW)
    )
    left_ref[...] = dot(place, jnp.concatenate(left_tiles, axis=0)).reshape(8, 8, LANE).astype(BF16)
    z_hi = lax.rem(lax.axis_index("depth"), 2)
    row, column = iotas(BLOCK, LANE)
    low = ones_where(row == column)
    high = ones_where(row + PAD == column)
    either = ones_where(row + PAD * z_hi == column)
    both = dot(t_ref[0], low) + dot(t_ref[1], high)
    t_out_ref[0] = both.reshape(GROUPS, 8, LANE).astype(BF16)
    t_out_ref[1] = dot(t_ref[2], either).reshape(GROUPS, 8, LANE).astype(BF16)


def place_of(row, col, depth):
    return row, depth // 2, (depth % 2) * 4 + col // 2, col % 2


def slot_of(x, y):
    return (y - x + 4) % 4 * 4 + x


def mesh_id(x, y, z, core):
    return {"row": x, "col": (z % 4) * 2 + core, "depth": y * 2 + z // 4}


def wait_bytes(ref, sem):
    pltpu.make_async_copy(ref, ref, sem).wait()


def exchange_kernel(
    f_ref, t_local, right_ref, left_ref, t_ref,
    send_ref, left_in, t_in, staged, bundle, relay, z_send, z_recv, xy_send, xy_recv,
    l_send, l_recv, t_send, t_recv, own_sem, z_own, xy_own,
):
    x, y, z, core = place_of(lax.axis_index("row"), lax.axis_index("col"), lax.axis_index("depth"))
    z_hi = z // 4
    active = slot_of(x, y) < SLOTS
    barrier = pltpu.get_barrier_semaphore()

    def greet(x, y, z, core):
        pl.semaphore_signal(
            barrier, inc=1, device_id=mesh_id(x, y, z, core), device_id_type=pl.DeviceIdType.MESH
        )

    @pl.loop(1, 16)
    def _(step):
        greet(x, y, (z + step) % 8, (core + step // 8) % 2)
        greet((x + step // 4) % 4, (y + step) % 4, z, core)

    prepare(f_ref, t_local, send_ref, left_in, t_in)
    pl.semaphore_wait(barrier, 30)
    half = LEFT_ROWS // 2

    def remote(src, dst, send, recv, to):
        return pltpu.make_async_remote_copy(
            src_ref=src, dst_ref=dst, send_sem=send, recv_sem=recv,
            device_id=mesh_id(*to), device_id_type=pl.DeviceIdType.MESH,
        )

    own_left = pltpu.make_async_copy(left_in, staged.at[z], own_sem.at[0])
    own_left.start()
    own_t = pltpu.make_async_copy(t_in.at[core], t_ref.at[core, y, z_hi, x], own_sem.at[1])
    own_t.start()
    remote(
        t_in.at[core], t_ref.at[core, y, z_hi, x], t_send.at[0], t_recv.at[0], (x, y, 7 - z, core)
    ).start()

    @pl.loop(1, 8)
    def _(step):
        remote(
            left_in, staged.at[z], l_send.at[0], l_recv.at[0], (x, y, (z + step) % 8, core)
        ).start()

    def width(part):
        return 1 if isinstance(ORDER[part], str) else 2

    def first_slot(part):
        if ORDER[part] == "own":
            return slot_of(x, y)
        if ORDER[part] == "beside":
            return slot_of(x, y) + 1 - 2 * (x % 2)
        diagonal, other = ORDER[part]
        return (y - x + diagonal + 4) % 4 * 4 + 2 * ((x // 2 + other) % 2)

    def by_count(part, act):
        short = first_slot(part) + width(part) > SLOTS
        if width(part) > 1:

            @pl.when(short)
            def _():
                act(width(part) - 1)

        @pl.when(jnp.logical_not(short))
        def _():
            act(width(part))

    def pair_at(to_z, to_core):
        return ACTIVE * (((to_z + 2) % 4) * 2 + to_core) + SLOTS * (to_z // 4)

    def send_along_z(part):
        first = first_slot(part)

        def send(count):
            @pl.loop(1, 16)
            def _(step):
                to_z, to_core = (z + step) % 8, (core + step // 8) % 2
                remote(
                    send_ref.at[pl.ds(pair_at(to_z, to_core) + first, count)],
                    relay.at[part, core, z, 0:count],
                    z_send.at[part], z_recv.at[part], (x, y, to_z, to_core),
                ).start()

            pltpu.make_async_copy(
                send_ref.at[pl.ds(pair_at(z, core) + first, count)],
                relay.at[part, core, z, 0:count],
                z_own.at[part],
            ).start()

        by_count(part, send)

    def pass_on(part):
        by_count(part, lambda count: wait_bytes(send_ref.at[0 : 15 * count], z_recv.at[part]))
        by_count(part, lambda count: wait_bytes(send_ref.at[0:count], z_own.at[part]))

        if ORDER[part] == "own":

            @pl.when(active)
            def _():
                pltpu.make_async_copy(
                    relay.at[part, :, :, 0], right_ref.at[:, x, y], xy_own
                ).start()

            return

        @pl.loop(0, width(part))
        def _(i):
            slot = first_slot(part) + i
            to_x = slot % 4

            @pl.when(slot < SLOTS)
            def _():
                remote(
                    relay.at[part, :, :, i], right_ref.at[:, x, y], xy_send.at[part],
                    xy_recv.at[part], (to_x, (to_x + slot // 4) % 4, z, core),
                ).start()

    send_along_z(0)
    send_along_z(1)

    own_left.wait()
    wait_bytes(staged.at[0:7], l_recv.at[0])
    out_row, in_row = iotas(64, 64)
    sort_rows = ones_where(in_row == ((out_row & 7) << 3) + (out_row >> 3))
    wide = jnp.concatenate(
        [staged[:, g].astype(F32).reshape(64, LANE) for g in range(8)], axis=1
    ).astype(BF16)
    wide = dot(sort_rows, wide)
    for g in range(8):
        block = wide[:, LANE * g : LANE * g + LANE].reshape(8, 8, LANE).astype(BF16)
        bundle[8 * g : 8 * g + 8] = block
    own_bundle = pltpu.make_async_copy(
        bundle.at[0:LEFT_ROWS], left_ref.at[:, core, x, y], own_sem.at[0]
    )
    own_bundle.start()
    own_t.wait()
    wait_bytes(t_ref.at[0, 0, 0, 0], t_recv.at[0])

    @pl.loop(1, 4)
    def _(step):
        remote(
            bundle.at[0:half], left_ref.at[0:half, core, x, y], l_send.at[1], l_recv.at[1],
            (x, (y + step) % 4, z, core),
        ).start()
        remote(
            bundle.at[half:LEFT_ROWS], left_ref.at[half:LEFT_ROWS, core, x, y],
            l_send.at[2], l_recv.at[2], ((x + step) % 4, y, z, core),
        ).start()
        block = t_ref.at[core, y, :, x]
        to = ((x + step * core) % 4, (y + step * (1 - core)) % 4, z, core)
        remote(block, block, t_send.at[1], t_recv.at[1], to).start()

    send_along_z(2)
    pass_on(0)
    send_along_z(3)

    own_bundle.wait()
    three_bundles = left_ref.at[0:half, 0, 0, 0:3]
    three_rings = left_ref.at[0:half, 0, 0:3]
    wait_bytes(three_bundles, l_recv.at[1])
    wait_bytes(three_bundles, l_recv.at[2])
    wait_bytes(t_ref.at[0, 0, :, 0:3], t_recv.at[1])

    @pl.loop(1, 4)
    def _(step):
        block = left_ref.at[0:half, core, x]
        remote(block, block, l_send.at[3], l_recv.at[3], ((x + step) % 4, y, z, core)).start()
        block = left_ref.at[half:LEFT_ROWS, core, :, y]
        remote(block, block, l_send.at[4], l_recv.at[4], (x, (y + step) % 4, z, core)).start()

        @pl.when(core == 0)
        def _():
            block = t_ref.at[0, :, :, x]
            remote(block, block, t_send.at[2], t_recv.at[2], ((x + step) % 4, y, z, core)).start()

        @pl.when(core == 1)
        def _():
            block = t_ref.at[1, y]
            remote(block, block, t_send.at[2], t_recv.at[2], (x, (y + step) % 4, z, core)).start()

    send_along_z(4)
    pass_on(1)
    send_along_z(5)
    pass_on(2)
    send_along_z(6)
    pass_on(3)
    send_along_z(7)
    send_along_z(8)

    wait_bytes(three_rings, l_recv.at[3])
    wait_bytes(three_rings, l_recv.at[4])
    sibling = (x, y, z, 1 - core)
    block = left_ref.at[:, core]
    swap_left = remote(block, block, l_send.at[5], l_recv.at[5], sibling)
    swap_left.start()
    wait_bytes(t_ref.at[0, 0:3], t_recv.at[2])
    block = t_ref.at[core]
    swap_t = remote(block, block, t_send.at[3], t_recv.at[3], sibling)
    swap_t.start()

    for part in range(4, PARTS):
        pass_on(part)

    swap_left.wait()
    swap_t.wait()
    wait_bytes(staged.at[0:7], l_send.at[0])
    wait_bytes(three_bundles, l_send.at[1])
    wait_bytes(three_bundles, l_send.at[2])
    wait_bytes(three_rings, l_send.at[3])
    wait_bytes(three_rings, l_send.at[4])
    wait_bytes(t_ref.at[0, 0, 0, 0], t_send.at[0])
    wait_bytes(t_ref.at[0, 0, :, 0:3], t_send.at[1])
    wait_bytes(t_ref.at[0, 0:3], t_send.at[2])

    for part in range(PARTS):
        by_count(part, lambda count: wait_bytes(send_ref.at[0 : 15 * count], z_send.at[part]))

    def columns(count):
        return right_ref.at[:, 0, 0:count]

    for part in range(PARTS - 1):
        by_count(part, lambda count: wait_bytes(columns(count), xy_send.at[part]))

    @pl.when(active)
    def _():
        wait_bytes(columns(1), xy_own)
        for part in range(PARTS - 1):
            wait_bytes(columns(width(part)), xy_recv.at[part])


def compute_kernel(
    right_ref, left_ref, t_ref, out_ref, right_n, right_t, mid, blocks, send_sem, recv_sem
):
    x, y, z, core = place_of(lax.axis_index("row"), lax.axis_index("col"), lax.axis_index("depth"))
    group = SLOTS * (z // 4) + slot_of(x, y)
    active = slot_of(x, y) < SLOTS
    barrier = pltpu.get_barrier_semaphore()

    def partner(step):
        return (x + step // 8) % 4, (y + step // 2) % 4, (z + 2 + 4 * (step % 2)) % 8

    @pl.loop(0, 32)
    def _(step):
        pl.semaphore_signal(
            barrier, inc=1, device_id=mesh_id(*partner(step), core),
            device_id_type=pl.DeviceIdType.MESH,
        )

    @pl.when(active)
    def _():
        out_row, in_row = iotas(256, 256)
        sort_rows = ones_where(in_row == ((out_row & 31) << 3) + (out_row >> 5))
        row, column = iotas(LANE, LANE)
        identity = ones_where(row == column)
        for q in range(Q_LOCAL):
            for chunk in range(0, 8, 2):
                block = jnp.concatenate(
                    [
                        right_ref[32 * c : 32 * c + 32, q].astype(F32).reshape(256, LANE)
                        for c in (chunk, chunk + 1)
                    ],
                    axis=1,
                )
                moved = dot(sort_rows, block.astype(BF16)).astype(BF16)
                for r in range(8):
                    for c in range(2):
                        base = 256 * q + 32 * (chunk + c)
                        right_n[r, base : base + 32, :] = moved[
                            32 * r : 32 * r + 32, LANE * c : LANE * c + LANE
                        ]
            for r in range(8):
                block = right_n[r, 256 * q : 256 * q + 256, :]
                right_t[LANE * r : LANE * r + LANE, 256 * q : 256 * q + 256] = dot_nt(
                    identity, block
                ).astype(BF16)
        for c in range(CW):
            left = jnp.concatenate(
                [
                    jnp.concatenate(
                        [
                            left_ref[12 * q + 4 * c + t].reshape(256, LANE)
                            for t in range(TILES)
                        ],
                        axis=1,
                    )
                    for q in range(Q_LOCAL)
                ],
                axis=0,
            )
            for m in range(4):
                which, half = divmod(m, 2)
                rebuilt = dot(right_t[256 * m : 256 * m + 256, :], left).astype(BF16)
                if c < 2:
                    for k in range(4):
                        base = (4 * half + k) * LANE + PAD * c
                        mid[which, base : base + PAD, :] = rebuilt[PAD * k : PAD * k + PAD]
                else:
                    base = 2 * NVP + 256 * half
                    mid[which, base : base + 256, :] = rebuilt

    pl.semaphore_wait(barrier, 32)

    @pl.when(active)
    def _():
        first_half = lax.broadcasted_iota(jnp.int32, (ROWS_P, LANE), 1) < PAD

        @pl.loop(0, 4)
        def _(turn):
            to_x = (x + turn) % 4

            def tile(kind, k):
                return t_ref[kind, k // 2, k % 2, to_x].astype(F32).reshape(ROWS_P, LANE)

            tiles = [tile(0, k) for k in range(BLOCKS)]
            tiles += [tile(1, 2 * k) + tile(1, 2 * k + 1) for k in range(4)]
            t_rows = jnp.concatenate(tiles, axis=1).astype(BF16)
            totals = [dot(t_rows, mid[which]) for which in range(2)]
            for k in range(4):
                lanes = slice(LANE * k, LANE * k + LANE)
                one, two = totals[0][:, lanes], totals[1][:, lanes]
                even = jnp.where(first_half, one, pltpu.roll(two, PAD, 1))
                odd = jnp.where(first_half, pltpu.roll(one, PAD, 1), two)
                blocks[to_x, 2 * k] = even.reshape(GROUPS, 8, LANE).astype(BF16)
                blocks[to_x, 2 * k + 1] = odd.reshape(GROUPS, 8, LANE).astype(BF16)

            @pl.loop(0, 8)
            def _(step):
                _, to_y, to_z = partner(step)
                pltpu.make_async_remote_copy(
                    src_ref=blocks.at[to_x, to_y * 2 + to_z // 4],
                    dst_ref=out_ref.at[group],
                    send_sem=send_sem,
                    recv_sem=recv_sem,
                    device_id=mesh_id(to_x, to_y, to_z, core),
                    device_id_type=pl.DeviceIdType.MESH,
                ).start()

    wait_bytes(out_ref.at[0:ACTIVE], recv_sem)

    @pl.when(active)
    def _():
        wait_bytes(blocks, send_sem)


def finish_kernel(in_ref, out_ref, turned):
    row, column = iotas(LANE, LANE)
    identity = ones_where(row == column)
    for group in range(ACTIVE):
        block = in_ref[group].astype(F32).reshape(ROWS_P, LANE).astype(BF16)
        turned[group] = dot_nt(identity, block)
    rows = 2 * ACTIVE * 8
    out_row, in_row = iotas(512, rows)
    sort_rows = ones_where(in_row == ((out_row & 63) << 3) + (out_row >> 6))
    for chunk in range(8):
        parts = []
        for group in range(ACTIVE):
            for which in range(2):
                base = PAD * which + 8 * chunk
                parts.append(turned[group, base : base + 8, :])
        moved = dot(sort_rows, jnp.concatenate(parts, axis=0).astype(BF16)).astype(BF16)
        for a in range(8 if chunk < 7 else 4):
            out_ref[8 * chunk + a] = moved[64 * a : 64 * a + 64][0:BLOCK, 0:ROWS_X]


def vmem(count):
    return [pl.BlockSpec(memory_space=pltpu.VMEM)] * count


def anywhere(count):
    return [pl.BlockSpec(memory_space=pl.ANY)] * count


def shape(*sizes):
    return jax.ShapeDtypeStruct(sizes, BF16)


def exchange(factors, amplitudes):
    dma = pltpu.SemaphoreType.DMA
    t_local = jnp.pad(amplitudes.transpose(1, 0, 2), ((0, 0), (0, ROWS_P - ROWS_X), (0, 0)))
    return pl.pallas_call(
        exchange_kernel,
        out_shape=(
            shape(2, 4, 4, 8, Q_LOCAL, 8, LANE),
            shape(LEFT_ROWS, 2, 4, 4, 8, LANE),
            shape(2, 4, 2, 4, GROUPS, 8, LANE),
        ),
        in_specs=vmem(2),
        out_specs=tuple(anywhere(3)),
        scratch_shapes=[
            pltpu.VMEM((B_PAIRS, Q_LOCAL, 8, LANE), BF16),
            pltpu.VMEM((8, 8, LANE), BF16),
            pltpu.VMEM((2, GROUPS, 8, LANE), BF16),
            pltpu.VMEM((8, 8, 8, LANE), BF16),
            pltpu.VMEM((64, 8, LANE), BF16),
            pltpu.VMEM((PARTS, 2, 8, 2, Q_LOCAL, 8, LANE), BF16),
            dma((PARTS,)), dma((PARTS,)), dma((PARTS,)), dma((PARTS,)),
            dma((6,)), dma((6,)), dma((4,)), dma((4,)), dma((2,)), dma((PARTS,)), dma,
        ],
        compiler_params=pltpu.CompilerParams(
            has_side_effects=True, vmem_limit_bytes=16 * MIB, collective_id=5
        ),
        name="exchange",
    )(factors, t_local)


def compute(right, left, t_full):
    dma = pltpu.SemaphoreType.DMA
    return pl.pallas_call(
        compute_kernel,
        out_shape=shape(32, GROUPS, 8, LANE),
        in_specs=vmem(3),
        out_specs=vmem(1)[0],
        scratch_shapes=[
            pltpu.VMEM((8, NAUX, LANE), BF16),
            pltpu.VMEM((2 * NVP, NAUX), BF16),
            pltpu.VMEM((2, KDIM, NVP), BF16),
            pltpu.VMEM((4, BLOCKS, GROUPS, 8, LANE), BF16),
            dma,
            dma,
        ],
        compiler_params=pltpu.CompilerParams(
            vmem_limit_bytes=28 * MIB, has_side_effects=True, collective_id=7
        ),
        name="compute",
    )(
        right.reshape(DEVICES, Q_LOCAL, 8, LANE),
        left.reshape(LEFT_ROWS, DEVICES // 8, 8, LANE),
        t_full,
    )


def finish(blocks):
    turned = pl.pallas_call(
        finish_kernel,
        out_shape=shape(BLOCK, BLOCK, ROWS_X),
        in_specs=vmem(1),
        out_specs=vmem(1)[0],
        scratch_shapes=[pltpu.VMEM((ACTIVE, LANE, ROWS_P), F32)],
        compiler_params=pltpu.CompilerParams(vmem_limit_bytes=40 * MIB),
        name="finish",
    )(blocks)
    return turned.transpose(2, 0, 1)


def on_device(factors, amplitudes):
    return finish(compute(*exchange(factors, amplitudes)))


def solution(mesh):
    in_specs = (P(("row", "col", "depth"), None, None), P("row", None, "depth"))
    out_specs = P("row", "depth", "col")
    return jax.shard_map(
        on_device, mesh=mesh, in_specs=in_specs, out_specs=out_specs, check_vma=False
    )
```

```python
import jax
import jax.numpy as jnp
from jax import lax
from jax.experimental import pallas as pl
from jax.experimental.pallas import tpu as pltpu
from jax.sharding import PartitionSpec as P

NV = 480
BLOCKS = 8
BLOCK = 60
PAD = 64
NVP = BLOCKS * PAD
LANE = 128
TILES = NVP // LANE
Q_LOCAL = 5
DEVICES = 256
NAUX = Q_LOCAL * DEVICES
CW = 3
ROWS_X = 132
GROUPS = 17
ROWS_P = GROUPS * 8
FOLD = 72
T_TILES = (GROUPS + FOLD // 8) // 2
B_PAIRS = 240
SLOTS = 15
ACTIVE = 2 * SLOTS
ORDER = ((2, 0), (2, 1), (1, 0), (1, 1), (3, 0), (3, 1), (0, 1), "beside", "own")
PARTS = len(ORDER)
GROUPED = (range(0, 5), range(5, 7), range(7, 9))
KDIM = CW * NVP
LEFT_ROWS = Q_LOCAL * CW * TILES
BF16 = jnp.bfloat16
F32 = jnp.float32
MIB = 1 << 20


def ones_where(mask):
    return jnp.where(mask, 1.0, 0.0).astype(BF16)


def iotas(rows, columns):
    shape = (rows, columns)
    return lax.broadcasted_iota(jnp.int32, shape, 0), lax.broadcasted_iota(jnp.int32, shape, 1)


def dot(left, right):
    return jnp.dot(left, right, preferred_element_type=F32)


def dot_nt(left, right):
    return lax.dot_general(left, right, (((1,), (1,)), ((), ())), preferred_element_type=F32)


def spread_matrix():
    row, column = iotas(NV, NVP)
    within = column & (PAD - 1)
    return ones_where((row == (column >> 6) * BLOCK + within) & (within < BLOCK))


def prepare(f_ref, t_ref, send_ref, left_ref, t_out_ref):
    spread = spread_matrix()
    out_row, in_row = iotas(LANE, LANE)
    gather_rows = ones_where(
        in_row == (out_row & 3) * 32 + (out_row >> 3) * 2 + ((out_row >> 2) & 1)
    )
    row, column = iotas(16, NV)
    pick = ones_where((row == column) & (row < CW))
    left_tiles = []
    for q in range(Q_LOCAL):
        wide = dot(f_ref[q], spread).astype(BF16)
        for chunk in range(NV // 32):
            rows = wide[32 * chunk : 32 * chunk + 32]
            stacked = jnp.concatenate(
                [rows[:, LANE * t : LANE * (t + 1)] for t in range(TILES)], axis=0
            )
            moved = dot(gather_rows, stacked).reshape(16, 8, LANE)
            send_ref[16 * chunk : 16 * chunk + 16, q] = moved.astype(BF16)
        picked = dot(dot_nt(pick, f_ref[q]).astype(BF16), spread).astype(BF16)
        left_tiles += [picked[:, LANE * t : LANE * (t + 1)] for t in range(TILES)]
    out_row, in_row = iotas(64, 64 * Q_LOCAL)
    place = ones_where(
        (out_row == (in_row >> 6) * 12 + (in_row & 15) * 4 + ((in_row >> 4) & 3))
        & ((in_row & 15) < CW)
    )
    left_ref[...] = dot(place, jnp.concatenate(left_tiles, axis=0)).reshape(8, 8, LANE).astype(BF16)
    row, column = iotas(BLOCK, LANE)
    low = ones_where(row == column)
    high = ones_where(row + PAD == column)
    both = (dot(t_ref[0], low) + dot(t_ref[1], high)).reshape(GROUPS, 8, LANE).astype(BF16)
    folded = dot(t_ref[2], low)[0:FOLD] + dot(t_ref[2], high)[ROWS_P - FOLD : ROWS_P]
    t_out_ref[0] = both[0:T_TILES]
    t_out_ref[1, 0 : GROUPS - T_TILES] = both[T_TILES:GROUPS]
    t_out_ref[1, GROUPS - T_TILES : T_TILES] = folded.reshape(FOLD // 8, 8, LANE).astype(BF16)


def place_of(row, col, depth):
    return row, depth // 2, (depth % 2) * 4 + col // 2, col % 2


def slot_of(x, y):
    return (y - x + 4) % 4 * 4 + x


def mesh_id(x, y, z, core):
    return {"row": x, "col": (z % 4) * 2 + core, "depth": y * 2 + z // 4}


def wait_bytes(ref, sem):
    pltpu.make_async_copy(ref, ref, sem).wait()


def ladder_kernel(
    f_ref, t_local, out_ref,
    send_ref, left_in, t_in, staged, bundle, relay, right_ref, left_ref, t_ref,
    left_rows, right_n, right_t, total, mid, blocks,
    z_send, z_recv, xy_send, xy_recv, l_send, l_recv, t_send, t_recv, own_sem, z_own, xy_own,
    out_send, out_recv,
):
    x, y, z, core = place_of(lax.axis_index("row"), lax.axis_index("col"), lax.axis_index("depth"))
    z_hi = z // 4
    active = slot_of(x, y) < SLOTS
    barrier = pltpu.get_barrier_semaphore()

    def greet(x, y, z, core):
        pl.semaphore_signal(
            barrier, inc=1, device_id=mesh_id(x, y, z, core), device_id_type=pl.DeviceIdType.MESH
        )

    @pl.loop(1, 16)
    def _(step):
        greet(x, y, (z + step) % 8, (core + step // 8) % 2)
        greet((x + step // 4) % 4, (y + step) % 4, z, core)
        greet((x + step // 4) % 4, (y + step) % 4, (z + 2) % 8, core)
        greet((x + step // 4) % 4, (y + step) % 4, (z + 6) % 8, core)

    prepare(f_ref, t_local, send_ref, left_in, t_in)
    pl.semaphore_wait(barrier, 60)
    half = LEFT_ROWS // 2

    def remote(src, dst, send, recv, to):
        return pltpu.make_async_remote_copy(
            src_ref=src, dst_ref=dst, send_sem=send, recv_sem=recv,
            device_id=mesh_id(*to), device_id_type=pl.DeviceIdType.MESH,
        )

    own_left = pltpu.make_async_copy(left_in, staged.at[z], own_sem.at[0])
    own_left.start()
    own_t = pltpu.make_async_copy(t_in.at[core], t_ref.at[core, y, z_hi, x], own_sem.at[1])
    own_t.start()
    remote(
        t_in.at[core], t_ref.at[core, y, z_hi, x], t_send.at[0], t_recv.at[0], (x, y, 7 - z, core)
    ).start()

    @pl.loop(1, 8)
    def _(step):
        remote(
            left_in, staged.at[z], l_send.at[0], l_recv.at[0], (x, y, (z + step) % 8, core)
        ).start()

    def width(part):
        return 1 if isinstance(ORDER[part], str) else 2

    def first_slot(part):
        if ORDER[part] == "own":
            return slot_of(x, y)
        if ORDER[part] == "beside":
            return slot_of(x, y) + 1 - 2 * (x % 2)
        diagonal, other = ORDER[part]
        return (y - x + diagonal + 4) % 4 * 4 + 2 * ((x // 2 + other) % 2)

    def by_count(part, act):
        short = first_slot(part) + width(part) > SLOTS
        if width(part) > 1:

            @pl.when(short)
            def _():
                act(width(part) - 1)

        @pl.when(jnp.logical_not(short))
        def _():
            act(width(part))

    def pair_at(to_z, to_core):
        return ACTIVE * (((to_z + 2) % 4) * 2 + to_core) + SLOTS * (to_z // 4)

    def send_along_z(part):
        first = first_slot(part)

        def send(count):
            @pl.loop(1, 16)
            def _(step):
                to_z, to_core = (z + step) % 8, (core + step // 8) % 2
                remote(
                    send_ref.at[pl.ds(pair_at(to_z, to_core) + first, count)],
                    relay.at[part, core, z, 0:count],
                    z_send.at[part], z_recv.at[part], (x, y, to_z, to_core),
                ).start()

            pltpu.make_async_copy(
                send_ref.at[pl.ds(pair_at(z, core) + first, count)],
                relay.at[part, core, z, 0:count],
                z_own.at[part],
            ).start()

        by_count(part, send)

    def pass_on(part):
        by_count(part, lambda count: wait_bytes(send_ref.at[0 : 15 * count], z_recv.at[part]))
        by_count(part, lambda count: wait_bytes(send_ref.at[0:count], z_own.at[part]))

        if ORDER[part] == "own":

            @pl.when(active)
            def _():
                pltpu.make_async_copy(
                    relay.at[part, :, :, 0], right_ref.at[x, y], xy_own
                ).start()

            return

        @pl.loop(0, width(part))
        def _(i):
            slot = first_slot(part) + i
            to_x = slot % 4

            @pl.when(slot < SLOTS)
            def _():
                remote(
                    relay.at[part, :, :, i], right_ref.at[x, y], xy_send.at[part],
                    xy_recv.at[part], (to_x, (to_x + slot // 4) % 4, z, core),
                ).start()

    send_along_z(0)
    send_along_z(1)

    own_left.wait()
    wait_bytes(staged.at[0:7], l_recv.at[0])
    out_row, in_row = iotas(64, 64)
    sort_rows = ones_where(in_row == ((out_row & 7) << 3) + (out_row >> 3))
    wide = jnp.concatenate(
        [staged[:, g].astype(F32).reshape(64, LANE) for g in range(8)], axis=1
    ).astype(BF16)
    wide = dot(sort_rows, wide)
    for g in range(8):
        block = wide[:, LANE * g : LANE * g + LANE].reshape(8, 8, LANE).astype(BF16)
        bundle[8 * g : 8 * g + 8] = block
    own_bundle = pltpu.make_async_copy(
        bundle.at[0:LEFT_ROWS], left_ref.at[:, x, y, core], own_sem.at[0]
    )
    own_bundle.start()
    own_t.wait()
    wait_bytes(t_ref.at[0, 0, 0, 0], t_recv.at[0])

    @pl.loop(1, 4)
    def _(step):
        remote(
            bundle.at[0:half], left_ref.at[0:half, x, y, core], l_send.at[1], l_recv.at[1],
            (x, (y + step) % 4, z, core),
        ).start()
        remote(
            bundle.at[half:LEFT_ROWS], left_ref.at[half:LEFT_ROWS, x, y, core],
            l_send.at[2], l_recv.at[2], ((x + step) % 4, y, z, core),
        ).start()
        block = t_ref.at[core, y, :, x]
        to = ((x + step * core) % 4, (y + step * (1 - core)) % 4, z, core)
        remote(block, block, t_send.at[1], t_recv.at[1], to).start()

    send_along_z(2)
    pass_on(0)
    send_along_z(3)

    own_bundle.wait()
    three_bundles = left_ref.at[0:half, 0, 0:3, 0]
    three_rings = left_ref.at[0:half, 0:3, :, 0]
    wait_bytes(three_bundles, l_recv.at[1])
    wait_bytes(three_bundles, l_recv.at[2])
    wait_bytes(t_ref.at[0, 0, :, 0:3], t_recv.at[1])

    @pl.loop(1, 4)
    def _(step):
        block = left_ref.at[0:half, x, :, core]
        remote(block, block, l_send.at[3], l_recv.at[3], ((x + step) % 4, y, z, core)).start()
        block = left_ref.at[half:LEFT_ROWS, :, y, core]
        remote(block, block, l_send.at[4], l_recv.at[4], (x, (y + step) % 4, z, core)).start()

        @pl.when(core == 0)
        def _():
            block = t_ref.at[0, :, :, x]
            remote(block, block, t_send.at[2], t_recv.at[2], ((x + step) % 4, y, z, core)).start()

        @pl.when(core == 1)
        def _():
            block = t_ref.at[1, y]
            remote(block, block, t_send.at[2], t_recv.at[2], (x, (y + step) % 4, z, core)).start()

    send_along_z(4)
    pass_on(1)
    send_along_z(5)
    pass_on(2)
    send_along_z(6)
    pass_on(3)
    send_along_z(7)
    send_along_z(8)

    wait_bytes(three_rings, l_recv.at[3])
    wait_bytes(three_rings, l_recv.at[4])
    sibling = (x, y, z, 1 - core)
    block = left_ref.at[:, :, :, core]
    swap_left = remote(block, block, l_send.at[5], l_recv.at[5], sibling)
    swap_left.start()
    wait_bytes(t_ref.at[0, 0:3], t_recv.at[2])
    block = t_ref.at[core]
    swap_t = remote(block, block, t_send.at[3], t_recv.at[3], sibling)
    swap_t.start()

    def columns(count):
        return right_ref.at[0, 0:count]

    out_row, in_row = iotas(256, 256)
    sort_rows = ones_where(in_row == ((out_row & 31) << 3) + (out_row >> 5))
    row, column = iotas(LANE, LANE)
    identity = ones_where(row == column)

    def sources(part):
        diagonal, other = (0, 0) if isinstance(ORDER[part], str) else ORDER[part]
        diagonal = (y - x - diagonal + 8) % 4
        from_x = 2 * ((x // 2 + other) % 2)
        return [(from_x + i, (from_x + i + diagonal) % 4) for i in range(2)]

    def pairs_of(group):
        return [part for part in GROUPED[group] if ORDER[part] != "own"]

    def sort_group(group):
        pairs = pairs_of(group)
        for chunk, part in enumerate(pairs):
            froms = sources(part)
            for q in range(Q_LOCAL):
                base = 32 * (Q_LOCAL * chunk + q)
                block = jnp.concatenate(
                    [
                        right_ref[from_x, from_y, :, :, q].astype(F32).reshape(LANE, LANE)
                        for from_x, from_y in froms
                    ],
                    axis=0,
                )
                moved = dot(sort_rows, block.astype(BF16)).astype(BF16)
                for r in range(8):
                    right_n[r, base : base + 32, :] = moved[32 * r : 32 * r + 32]
        depth = 32 * Q_LOCAL * len(pairs)
        for r in range(8):
            right_t[LANE * r : LANE * r + LANE, 0:depth] = dot_nt(
                identity, right_n[r, 0:depth, :]
            ).astype(BF16)

    def gather_left(group):
        for chunk, part in enumerate(pairs_of(group)):
            for i, (from_x, from_y) in enumerate(sources(part)):
                for r in range(LEFT_ROWS):
                    q, tile = divmod(r, CW * TILES)
                    base = 32 * (Q_LOCAL * chunk + q) + 16 * i
                    left_rows[base : base + 16, LANE * tile : LANE * tile + LANE] = left_ref[
                        r, from_x, from_y
                    ].reshape(16, LANE)

    def multiply(group):
        depth = 32 * Q_LOCAL * len(pairs_of(group))
        for m in range(4):
            which, half_of_d = divmod(m, 2)
            for c in range(CW):
                rows, lanes = slice(256 * m, 256 * m + 256), slice(NVP * c, NVP * c + NVP)
                rebuilt = dot(right_t[rows, 0:depth], left_rows[0:depth, lanes])
                if group > 0:
                    rebuilt += total[rows, lanes]
                if group < len(GROUPED) - 1:
                    total[rows, lanes] = rebuilt
                    continue
                rebuilt = rebuilt.astype(BF16)
                if c < 2:
                    for k in range(4):
                        base = (4 * half_of_d + k) * LANE + PAD * c
                        mid[which, base : base + PAD, :] = rebuilt[PAD * k : PAD * k + PAD]
                else:
                    base = 2 * NVP + 256 * half_of_d
                    mid[which, base : base + 256, :] = rebuilt

    def arrived(parts):
        for part in parts:
            if ORDER[part] == "own":
                wait_bytes(columns(1), xy_own)
            else:
                wait_bytes(columns(width(part)), xy_recv.at[part])

    pass_on(4)
    pass_on(5)

    @pl.when(active)
    def _():
        arrived(GROUPED[0])
        sort_group(0)

    pass_on(6)
    swap_left.wait_recv()

    @pl.when(active)
    def _():
        gather_left(0)
        multiply(0)

    pass_on(7)

    @pl.when(active)
    def _():
        arrived(GROUPED[1])
        sort_group(1)
        gather_left(1)
        multiply(1)

    pass_on(8)
    swap_t.wait_recv()
    slot = SLOTS * z_hi + slot_of(x, y)

    @pl.when(active)
    def _():
        gather_left(2)
        arrived(GROUPED[2])
        sort_group(2)
        multiply(2)
        first_half = lax.broadcasted_iota(jnp.int32, (ROWS_P, LANE), 1) < PAD

        @pl.loop(0, 4)
        def _(turn):
            to_x = (x + turn) % 4

            def tiles_of(half, k, first, last):
                return t_ref[half, k // 2, k % 2, to_x, first:last].astype(F32)

            def side_by_side(k):
                rest = GROUPS - T_TILES
                whole = [tiles_of(0, k, 0, T_TILES), tiles_of(1, k, 0, rest)]
                return jnp.concatenate(whole, axis=0).reshape(ROWS_P, LANE)

            def unfolded(k):
                one, two = (
                    tiles_of(1, k + i, GROUPS - T_TILES, T_TILES).reshape(FOLD, LANE)
                    for i in range(2)
                )
                begin = first_half[0:FOLD]
                top = jnp.where(begin, one, pltpu.roll(two, PAD, 1))
                bottom = jnp.where(begin, pltpu.roll(one, PAD, 1), two)
                return jnp.concatenate([top, bottom[2 * FOLD - ROWS_P : FOLD]], axis=0)

            tiles = [side_by_side(k) for k in range(BLOCKS)]
            tiles += [unfolded(2 * k) for k in range(4)]
            t_rows = jnp.concatenate(tiles, axis=1).astype(BF16)
            totals = [dot(t_rows, mid[which]) for which in range(2)]
            for k in range(4):
                lanes = slice(LANE * k, LANE * k + LANE)
                one, two = totals[0][:, lanes], totals[1][:, lanes]
                even = jnp.where(first_half, one, pltpu.roll(two, PAD, 1))
                odd = jnp.where(first_half, pltpu.roll(one, PAD, 1), two)
                blocks[to_x, 2 * k] = even.reshape(GROUPS, 8, LANE).astype(BF16)
                blocks[to_x, 2 * k + 1] = odd.reshape(GROUPS, 8, LANE).astype(BF16)

            @pl.loop(0, 8)
            def _(step):
                to_y, to_z = (y + step // 2) % 4, (z + 2 + 4 * (step % 2)) % 8
                pltpu.make_async_remote_copy(
                    src_ref=blocks.at[to_x, to_y * 2 + to_z // 4],
                    dst_ref=out_ref.at[slot],
                    send_sem=out_send,
                    recv_sem=out_recv,
                    device_id=mesh_id(to_x, to_y, to_z, core),
                    device_id_type=pl.DeviceIdType.MESH,
                ).start()

    wait_bytes(out_ref.at[0:ACTIVE], out_recv)

    @pl.when(active)
    def _():
        wait_bytes(blocks, out_send)

    swap_left.wait_send()
    swap_t.wait_send()
    wait_bytes(staged.at[0:7], l_send.at[0])
    wait_bytes(three_bundles, l_send.at[1])
    wait_bytes(three_bundles, l_send.at[2])
    wait_bytes(three_rings, l_send.at[3])
    wait_bytes(three_rings, l_send.at[4])
    wait_bytes(t_ref.at[0, 0, 0, 0], t_send.at[0])
    wait_bytes(t_ref.at[0, 0, :, 0:3], t_send.at[1])
    wait_bytes(t_ref.at[0, 0:3], t_send.at[2])

    for part in range(PARTS):
        by_count(part, lambda count: wait_bytes(send_ref.at[0 : 15 * count], z_send.at[part]))

    for part in range(PARTS - 1):
        by_count(part, lambda count: wait_bytes(columns(count), xy_send.at[part]))

def finish_kernel(in_ref, out_ref, turned):
    row, column = iotas(LANE, LANE)
    identity = ones_where(row == column)
    for group in range(ACTIVE):
        block = in_ref[group].astype(F32).reshape(ROWS_P, LANE).astype(BF16)
        turned[group] = dot_nt(identity, block)
    rows = 2 * ACTIVE * 8
    out_row, in_row = iotas(512, rows)
    sort_rows = ones_where(in_row == ((out_row & 63) << 3) + (out_row >> 6))
    for chunk in range(8):
        parts = []
        for group in range(ACTIVE):
            for which in range(2):
                base = PAD * which + 8 * chunk
                parts.append(turned[group, base : base + 8, :])
        moved = dot(sort_rows, jnp.concatenate(parts, axis=0).astype(BF16)).astype(BF16)
        for a in range(8 if chunk < 7 else 4):
            out_ref[8 * chunk + a] = moved[64 * a : 64 * a + 64][0:BLOCK, 0:ROWS_X]


def vmem(count):
    return [pl.BlockSpec(memory_space=pltpu.VMEM)] * count


def anywhere(count):
    return [pl.BlockSpec(memory_space=pl.ANY)] * count


def shape(*sizes):
    return jax.ShapeDtypeStruct(sizes, BF16)


def ladder(factors, amplitudes):
    dma = pltpu.SemaphoreType.DMA
    t_local = jnp.pad(amplitudes.transpose(1, 0, 2), ((0, 0), (0, ROWS_P - ROWS_X), (0, 0)))
    deepest = 32 * Q_LOCAL * 5
    return pl.pallas_call(
        ladder_kernel,
        out_shape=shape(32, GROUPS, 8, LANE),
        in_specs=vmem(2),
        out_specs=vmem(1)[0],
        scratch_shapes=[
            pltpu.VMEM((B_PAIRS, Q_LOCAL, 8, LANE), BF16),
            pltpu.VMEM((8, 8, LANE), BF16),
            pltpu.VMEM((2, T_TILES, 8, LANE), BF16),
            pltpu.VMEM((8, 8, 8, LANE), BF16),
            pltpu.VMEM((64, 8, LANE), BF16),
            pltpu.VMEM((PARTS, 2, 8, 2, Q_LOCAL, 8, LANE), BF16),
            pltpu.VMEM((4, 4, 2, 8, Q_LOCAL, 8, LANE), BF16),
            pltpu.VMEM((LEFT_ROWS, 4, 4, 2, 8, LANE), BF16),
            pltpu.VMEM((2, 4, 2, 4, T_TILES, 8, LANE), BF16),
            pltpu.VMEM((deepest, KDIM), BF16),
            pltpu.VMEM((8, deepest, LANE), BF16),
            pltpu.VMEM((2 * NVP, deepest + 96), BF16),
            pltpu.VMEM((2 * NVP, KDIM), F32),
            pltpu.VMEM((2, KDIM, NVP), BF16),
            pltpu.VMEM((4, BLOCKS, GROUPS, 8, LANE), BF16),
            dma((PARTS,)), dma((PARTS,)), dma((PARTS,)), dma((PARTS,)),
            dma((6,)), dma((6,)), dma((4,)), dma((4,)), dma((2,)), dma((PARTS,)), dma,
            dma, dma,
        ],
        compiler_params=pltpu.CompilerParams(
            has_side_effects=True, vmem_limit_bytes=42 * MIB, collective_id=5
        ),
        name="ladder",
    )(factors, t_local)


def finish(blocks):
    turned = pl.pallas_call(
        finish_kernel,
        out_shape=shape(BLOCK, BLOCK, ROWS_X),
        in_specs=vmem(1),
        out_specs=vmem(1)[0],
        scratch_shapes=[pltpu.VMEM((ACTIVE, LANE, ROWS_P), F32)],
        compiler_params=pltpu.CompilerParams(vmem_limit_bytes=40 * MIB),
        name="finish",
    )(blocks)
    return turned.transpose(2, 0, 1)


def on_device(factors, amplitudes):
    return finish(ladder(factors, amplitudes))


def solution(mesh):
    in_specs = (P(("row", "col", "depth"), None, None), P("row", None, "depth"))
    out_specs = P("row", "depth", "col")
    return jax.shard_map(
        on_device, mesh=mesh, in_specs=in_specs, out_specs=out_specs, check_vma=False
    )
```

```python
import jax
import jax.numpy as jnp
from jax import lax
from jax.experimental import pallas as pl
from jax.experimental.pallas import tpu as pltpu
from jax.sharding import PartitionSpec as P

NV = 480
BLOCKS = 8
BLOCK = 60
PAD = 64
NVP = BLOCKS * PAD
LANE = 128
TILES = NVP // LANE
Q_LOCAL = 5
DEVICES = 256
NAUX = Q_LOCAL * DEVICES
CW = 3
ROWS_X = 132
GROUPS = 17
ROWS_P = GROUPS * 8
FOLD = 72
T_TILES = (GROUPS + FOLD // 8) // 2
B_PAIRS = 240
SLOTS = 15
ACTIVE = 2 * SLOTS
ORDER = ((2, 0), (2, 1), (1, 0), (1, 1), (3, 0), (3, 1), (0, 1), "beside", "own")
PARTS = len(ORDER)
GROUPED = (range(0, 5), range(5, 7), range(7, 9))
KDIM = CW * NVP
LEFT_ROWS = Q_LOCAL * CW * TILES
BF16 = jnp.bfloat16
F32 = jnp.float32
MIB = 1 << 20


def ones_where(mask):
    return jnp.where(mask, 1.0, 0.0).astype(BF16)


def iotas(rows, columns):
    shape = (rows, columns)
    return lax.broadcasted_iota(jnp.int32, shape, 0), lax.broadcasted_iota(jnp.int32, shape, 1)


def dot(left, right):
    return jnp.dot(left, right, preferred_element_type=F32)


def dot_nt(left, right):
    return lax.dot_general(left, right, (((1,), (1,)), ((), ())), preferred_element_type=F32)


def spread_matrix():
    row, column = iotas(NV, NVP)
    within = column & (PAD - 1)
    return ones_where((row == (column >> 6) * BLOCK + within) & (within < BLOCK))


def prepare(f_ref, t_ref, send_ref, left_ref, t_out_ref):
    spread = spread_matrix()
    out_row, in_row = iotas(LANE, LANE)
    gather_rows = ones_where(
        in_row == (out_row & 3) * 32 + (out_row >> 3) * 2 + ((out_row >> 2) & 1)
    )
    row, column = iotas(16, NV)
    pick = ones_where((row == column) & (row < CW))
    left_tiles = []
    for q in range(Q_LOCAL):
        wide = dot(f_ref[q], spread).astype(BF16)
        for chunk in range(NV // 32):
            rows = wide[32 * chunk : 32 * chunk + 32]
            stacked = jnp.concatenate(
                [rows[:, LANE * t : LANE * (t + 1)] for t in range(TILES)], axis=0
            )
            moved = dot(gather_rows, stacked).reshape(16, 8, LANE)
            send_ref[16 * chunk : 16 * chunk + 16, q] = moved.astype(BF16)
        picked = dot(dot_nt(pick, f_ref[q]).astype(BF16), spread).astype(BF16)
        left_tiles += [picked[:, LANE * t : LANE * (t + 1)] for t in range(TILES)]
    out_row, in_row = iotas(64, 64 * Q_LOCAL)
    place = ones_where(
        (out_row == (in_row >> 6) * 12 + (in_row & 15) * 4 + ((in_row >> 4) & 3))
        & ((in_row & 15) < CW)
    )
    left_ref[...] = dot(place, jnp.concatenate(left_tiles, axis=0)).reshape(8, 8, LANE).astype(BF16)
    row, column = iotas(BLOCK, LANE)
    low = ones_where(row == column)
    high = ones_where(row + PAD == column)
    both = (dot(t_ref[0], low) + dot(t_ref[1], high)).reshape(GROUPS, 8, LANE).astype(BF16)
    folded = dot(t_ref[2], low)[0:FOLD] + dot(t_ref[2], high)[ROWS_P - FOLD : ROWS_P]
    t_out_ref[0] = both[0:T_TILES]
    t_out_ref[1, 0 : GROUPS - T_TILES] = both[T_TILES:GROUPS]
    t_out_ref[1, GROUPS - T_TILES : T_TILES] = folded.reshape(FOLD // 8, 8, LANE).astype(BF16)


def place_of(row, col, depth):
    return row, depth // 2, (depth % 2) * 4 + col // 2, col % 2


def slot_of(x, y):
    return (y - x + 4) % 4 * 4 + x


def mesh_id(x, y, z, core):
    return {"row": x, "col": (z % 4) * 2 + core, "depth": y * 2 + z // 4}


def wait_bytes(ref, sem):
    pltpu.make_async_copy(ref, ref, sem).wait()


def ladder_kernel(
    f_ref, t_local, out_ref,
    send_ref, left_in, t_in, staged, bundle, relay, right_ref, left_ref, t_ref,
    left_rows, right_n, right_t, total, mid, blocks,
    z_send, z_recv, xy_send, xy_recv, l_send, l_recv, t_send, t_recv, own_sem, z_own, xy_own,
    out_send, out_recv,
):
    x, y, z, core = place_of(lax.axis_index("row"), lax.axis_index("col"), lax.axis_index("depth"))
    z_hi = z // 4
    active = slot_of(x, y) < SLOTS
    barrier = pltpu.get_barrier_semaphore()

    def greet(x, y, z, core):
        pl.semaphore_signal(
            barrier, inc=1, device_id=mesh_id(x, y, z, core), device_id_type=pl.DeviceIdType.MESH
        )

    @pl.loop(1, 16)
    def _(step):
        greet(x, y, (z + step) % 8, (core + step // 8) % 2)
        greet((x + step // 4) % 4, (y + step) % 4, z, core)
        greet((x + step // 4) % 4, (y + step) % 4, (z + 2) % 8, core)
        greet((x + step // 4) % 4, (y + step) % 4, (z + 6) % 8, core)

    prepare(f_ref, t_local, send_ref, left_in, t_in)
    pl.semaphore_wait(barrier, 60)
    half = LEFT_ROWS // 2

    def remote(src, dst, send, recv, to):
        return pltpu.make_async_remote_copy(
            src_ref=src, dst_ref=dst, send_sem=send, recv_sem=recv,
            device_id=mesh_id(*to), device_id_type=pl.DeviceIdType.MESH,
        )

    own_left = pltpu.make_async_copy(left_in, staged.at[z], own_sem.at[0])
    own_left.start()
    own_t = pltpu.make_async_copy(t_in.at[core], t_ref.at[core, y, z_hi, x], own_sem.at[1])
    own_t.start()
    remote(
        t_in.at[core], t_ref.at[core, y, z_hi, x], t_send.at[0], t_recv.at[0], (x, y, 7 - z, core)
    ).start()

    @pl.loop(1, 8)
    def _(step):
        remote(
            left_in, staged.at[z], l_send.at[0], l_recv.at[0], (x, y, (z + step) % 8, core)
        ).start()

    def width(part):
        return 1 if isinstance(ORDER[part], str) else 2

    def first_slot(part):
        if ORDER[part] == "own":
            return slot_of(x, y)
        if ORDER[part] == "beside":
            return slot_of(x, y) + 1 - 2 * (x % 2)
        diagonal, other = ORDER[part]
        return (y - x + diagonal + 4) % 4 * 4 + 2 * ((x // 2 + other) % 2)

    def by_count(part, act):
        short = first_slot(part) + width(part) > SLOTS
        if width(part) > 1:

            @pl.when(short)
            def _():
                act(width(part) - 1)

        @pl.when(jnp.logical_not(short))
        def _():
            act(width(part))

    def pair_at(to_z, to_core):
        return ACTIVE * (((to_z + 2) % 4) * 2 + to_core) + SLOTS * (to_z // 4)

    def send_along_z(part):
        first = first_slot(part)

        def send(count):
            @pl.loop(1, 16)
            def _(step):
                to_z, to_core = (z + step) % 8, (core + step // 8) % 2
                remote(
                    send_ref.at[pl.ds(pair_at(to_z, to_core) + first, count)],
                    relay.at[part, core, z, 0:count],
                    z_send.at[part], z_recv.at[part], (x, y, to_z, to_core),
                ).start()

            pltpu.make_async_copy(
                send_ref.at[pl.ds(pair_at(z, core) + first, count)],
                relay.at[part, core, z, 0:count],
                z_own.at[part],
            ).start()

        by_count(part, send)

    def pass_on(part):
        by_count(part, lambda count: wait_bytes(send_ref.at[0 : 15 * count], z_recv.at[part]))
        by_count(part, lambda count: wait_bytes(send_ref.at[0:count], z_own.at[part]))

        if ORDER[part] == "own":

            @pl.when(active)
            def _():
                pltpu.make_async_copy(
                    relay.at[part, :, :, 0], right_ref.at[x, y], xy_own
                ).start()

            return

        @pl.loop(0, width(part))
        def _(i):
            slot = first_slot(part) + i
            to_x = slot % 4

            @pl.when(slot < SLOTS)
            def _():
                remote(
                    relay.at[part, :, :, i], right_ref.at[x, y], xy_send.at[part],
                    xy_recv.at[part], (to_x, (to_x + slot // 4) % 4, z, core),
                ).start()

    send_along_z(0)
    send_along_z(1)

    own_left.wait()
    wait_bytes(staged.at[0:7], l_recv.at[0])
    out_row, in_row = iotas(64, 64)
    sort_rows = ones_where(in_row == ((out_row & 7) << 3) + (out_row >> 3))
    wide = jnp.concatenate(
        [staged[:, g].astype(F32).reshape(64, LANE) for g in range(8)], axis=1
    ).astype(BF16)
    wide = dot(sort_rows, wide)
    for g in range(8):
        block = wide[:, LANE * g : LANE * g + LANE].reshape(8, 8, LANE).astype(BF16)
        bundle[8 * g : 8 * g + 8] = block
    own_bundle = pltpu.make_async_copy(
        bundle.at[0:LEFT_ROWS], left_ref.at[:, x, y, core], own_sem.at[0]
    )
    own_bundle.start()
    own_t.wait()
    wait_bytes(t_ref.at[0, 0, 0, 0], t_recv.at[0])

    @pl.loop(1, 4)
    def _(step):
        remote(
            bundle.at[0:half], left_ref.at[0:half, x, y, core], l_send.at[1], l_recv.at[1],
            (x, (y + step) % 4, z, core),
        ).start()
        remote(
            bundle.at[half:LEFT_ROWS], left_ref.at[half:LEFT_ROWS, x, y, core],
            l_send.at[2], l_recv.at[2], ((x + step) % 4, y, z, core),
        ).start()
        block = t_ref.at[core, y, :, x]
        to = ((x + step * core) % 4, (y + step * (1 - core)) % 4, z, core)
        remote(block, block, t_send.at[1], t_recv.at[1], to).start()

    send_along_z(2)
    pass_on(0)
    send_along_z(3)

    own_bundle.wait()
    three_bundles = left_ref.at[0:half, 0, 0:3, 0]
    three_rings = left_ref.at[0:half, 0:3, :, 0]
    wait_bytes(three_bundles, l_recv.at[1])
    wait_bytes(three_bundles, l_recv.at[2])
    wait_bytes(t_ref.at[0, 0, :, 0:3], t_recv.at[1])

    @pl.loop(1, 4)
    def _(step):
        block = left_ref.at[0:half, x, :, core]
        remote(block, block, l_send.at[3], l_recv.at[3], ((x + step) % 4, y, z, core)).start()
        block = left_ref.at[half:LEFT_ROWS, :, y, core]
        remote(block, block, l_send.at[4], l_recv.at[4], (x, (y + step) % 4, z, core)).start()

        @pl.when(core == 0)
        def _():
            block = t_ref.at[0, :, :, x]
            remote(block, block, t_send.at[2], t_recv.at[2], ((x + step) % 4, y, z, core)).start()

        @pl.when(core == 1)
        def _():
            block = t_ref.at[1, y]
            remote(block, block, t_send.at[2], t_recv.at[2], (x, (y + step) % 4, z, core)).start()

    send_along_z(4)
    pass_on(1)
    send_along_z(5)
    pass_on(2)
    send_along_z(6)
    pass_on(3)
    send_along_z(7)
    send_along_z(8)

    wait_bytes(three_rings, l_recv.at[3])
    wait_bytes(three_rings, l_recv.at[4])
    sibling = (x, y, z, 1 - core)
    block = left_ref.at[:, :, :, core]
    swap_left = remote(block, block, l_send.at[5], l_recv.at[5], sibling)
    swap_left.start()
    wait_bytes(t_ref.at[0, 0:3], t_recv.at[2])
    block = t_ref.at[core]
    swap_t = remote(block, block, t_send.at[3], t_recv.at[3], sibling)
    swap_t.start()

    def columns(count):
        return right_ref.at[0, 0:count]

    out_row, in_row = iotas(256, 256)
    sort_rows = ones_where(in_row == ((out_row & 31) << 3) + (out_row >> 5))
    row, column = iotas(LANE, LANE)
    identity = ones_where(row == column)

    def sources(part):
        diagonal, other = (0, 0) if isinstance(ORDER[part], str) else ORDER[part]
        diagonal = (y - x - diagonal + 8) % 4
        from_x = 2 * ((x // 2 + other) % 2)
        return [(from_x + i, (from_x + i + diagonal) % 4) for i in range(2)]

    def pairs_of(group):
        return [part for part in GROUPED[group] if ORDER[part] != "own"]

    def sort_group(group):
        pairs = pairs_of(group)
        for chunk, part in enumerate(pairs):
            froms = sources(part)
            for q in range(Q_LOCAL):
                base = 32 * (Q_LOCAL * chunk + q)
                block = jnp.concatenate(
                    [
                        right_ref[from_x, from_y, :, :, q].astype(F32).reshape(LANE, LANE)
                        for from_x, from_y in froms
                    ],
                    axis=0,
                )
                moved = dot(sort_rows, block.astype(BF16)).astype(BF16)
                for r in range(8):
                    right_n[r, base : base + 32, :] = moved[32 * r : 32 * r + 32]
        depth = 32 * Q_LOCAL * len(pairs)
        for r in range(8):
            right_t[LANE * r : LANE * r + LANE, 0:depth] = dot_nt(
                identity, right_n[r, 0:depth, :]
            ).astype(BF16)

    def gather_left(group):
        for chunk, part in enumerate(pairs_of(group)):
            for i, (from_x, from_y) in enumerate(sources(part)):
                for r in range(LEFT_ROWS):
                    q, tile = divmod(r, CW * TILES)
                    base = 32 * (Q_LOCAL * chunk + q) + 16 * i
                    left_rows[base : base + 16, LANE * tile : LANE * tile + LANE] = left_ref[
                        r, from_x, from_y
                    ].reshape(16, LANE)

    def multiply(group):
        depth = 32 * Q_LOCAL * len(pairs_of(group))
        for m in range(4):
            which, half_of_d = divmod(m, 2)
            for c in range(CW):
                rows, lanes = slice(256 * m, 256 * m + 256), slice(NVP * c, NVP * c + NVP)
                rebuilt = dot(right_t[rows, 0:depth], left_rows[0:depth, lanes])
                if group > 0:
                    rebuilt += total[rows, lanes]
                if group < len(GROUPED) - 1:
                    total[rows, lanes] = rebuilt
                    continue
                rebuilt = rebuilt.astype(BF16)
                if c < 2:
                    for k in range(4):
                        base = (4 * half_of_d + k) * LANE + PAD * c
                        mid[which, base : base + PAD, :] = rebuilt[PAD * k : PAD * k + PAD]
                else:
                    base = 2 * NVP + 256 * half_of_d
                    mid[which, base : base + 256, :] = rebuilt

    def arrived(parts):
        for part in parts:
            if ORDER[part] == "own":
                wait_bytes(columns(1), xy_own)
            else:
                wait_bytes(columns(width(part)), xy_recv.at[part])

    pass_on(4)
    pass_on(5)

    @pl.when(active)
    def _():
        arrived(GROUPED[0])
        sort_group(0)

    pass_on(6)
    swap_left.wait_recv()

    @pl.when(active)
    def _():
        gather_left(0)
        multiply(0)

    pass_on(7)

    @pl.when(active)
    def _():
        arrived(GROUPED[1])
        sort_group(1)
        gather_left(1)
        multiply(1)

    pass_on(8)
    swap_t.wait_recv()
    slot = SLOTS * z_hi + slot_of(x, y)

    @pl.when(active)
    def _():
        gather_left(2)
        arrived(GROUPED[2])
        sort_group(2)
        multiply(2)
        first_half = lax.broadcasted_iota(jnp.int32, (ROWS_P, LANE), 1) < PAD

        @pl.loop(0, 4)
        def _(turn):
            to_x = (x + 2 + turn) % 4

            def tiles_of(half, k, first, last):
                return t_ref[half, k // 2, k % 2, to_x, first:last].astype(F32)

            def side_by_side(k):
                rest = GROUPS - T_TILES
                whole = [tiles_of(0, k, 0, T_TILES), tiles_of(1, k, 0, rest)]
                return jnp.concatenate(whole, axis=0).reshape(ROWS_P, LANE)

            def unfolded(k):
                one, two = (
                    tiles_of(1, k + i, GROUPS - T_TILES, T_TILES).reshape(FOLD, LANE)
                    for i in range(2)
                )
                begin = first_half[0:FOLD]
                top = jnp.where(begin, one, pltpu.roll(two, PAD, 1))
                bottom = jnp.where(begin, pltpu.roll(one, PAD, 1), two)
                return jnp.concatenate([top, bottom[2 * FOLD - ROWS_P : FOLD]], axis=0)

            tiles = [side_by_side(k) for k in range(BLOCKS)]
            tiles += [unfolded(2 * k) for k in range(4)]
            t_rows = jnp.concatenate(tiles, axis=1).astype(BF16)
            totals = [dot(t_rows, mid[which]) for which in range(2)]
            for k in range(4):
                lanes = slice(LANE * k, LANE * k + LANE)
                one, two = totals[0][:, lanes], totals[1][:, lanes]
                even = jnp.where(first_half, one, pltpu.roll(two, PAD, 1))
                odd = jnp.where(first_half, pltpu.roll(one, PAD, 1), two)
                blocks[to_x, 2 * k] = even.reshape(GROUPS, 8, LANE).astype(BF16)
                blocks[to_x, 2 * k + 1] = odd.reshape(GROUPS, 8, LANE).astype(BF16)

            @pl.loop(0, 8)
            def _(step):
                to_y, to_z = (y + step // 2) % 4, (z + 2 + 4 * (step % 2)) % 8
                pltpu.make_async_remote_copy(
                    src_ref=blocks.at[to_x, to_y * 2 + to_z // 4],
                    dst_ref=out_ref.at[slot],
                    send_sem=out_send,
                    recv_sem=out_recv,
                    device_id=mesh_id(to_x, to_y, to_z, core),
                    device_id_type=pl.DeviceIdType.MESH,
                ).start()

    wait_bytes(out_ref.at[0:ACTIVE], out_recv)

    @pl.when(active)
    def _():
        wait_bytes(blocks, out_send)

    swap_left.wait_send()
    swap_t.wait_send()
    wait_bytes(staged.at[0:7], l_send.at[0])
    wait_bytes(three_bundles, l_send.at[1])
    wait_bytes(three_bundles, l_send.at[2])
    wait_bytes(three_rings, l_send.at[3])
    wait_bytes(three_rings, l_send.at[4])
    wait_bytes(t_ref.at[0, 0, 0, 0], t_send.at[0])
    wait_bytes(t_ref.at[0, 0, :, 0:3], t_send.at[1])
    wait_bytes(t_ref.at[0, 0:3], t_send.at[2])

    for part in range(PARTS):
        by_count(part, lambda count: wait_bytes(send_ref.at[0 : 15 * count], z_send.at[part]))

    for part in range(PARTS - 1):
        by_count(part, lambda count: wait_bytes(columns(count), xy_send.at[part]))

def finish_kernel(in_ref, out_ref, turned):
    row, column = iotas(LANE, LANE)
    identity = ones_where(row == column)
    for group in range(ACTIVE):
        block = in_ref[group].astype(F32).reshape(ROWS_P, LANE).astype(BF16)
        turned[group] = dot_nt(identity, block)
    rows = 2 * ACTIVE * 8
    out_row, in_row = iotas(512, rows)
    sort_rows = ones_where(in_row == ((out_row & 63) << 3) + (out_row >> 6))
    for chunk in range(8):
        parts = []
        for group in range(ACTIVE):
            for which in range(2):
                base = PAD * which + 8 * chunk
                parts.append(turned[group, base : base + 8, :])
        moved = dot(sort_rows, jnp.concatenate(parts, axis=0).astype(BF16)).astype(BF16)
        for a in range(8 if chunk < 7 else 4):
            out_ref[8 * chunk + a] = moved[64 * a : 64 * a + 64][0:BLOCK, 0:ROWS_X]


def vmem(count):
    return [pl.BlockSpec(memory_space=pltpu.VMEM)] * count


def anywhere(count):
    return [pl.BlockSpec(memory_space=pl.ANY)] * count


def shape(*sizes):
    return jax.ShapeDtypeStruct(sizes, BF16)


def ladder(factors, amplitudes):
    dma = pltpu.SemaphoreType.DMA
    t_local = jnp.pad(amplitudes.transpose(1, 0, 2), ((0, 0), (0, ROWS_P - ROWS_X), (0, 0)))
    deepest = 32 * Q_LOCAL * 5
    return pl.pallas_call(
        ladder_kernel,
        out_shape=shape(32, GROUPS, 8, LANE),
        in_specs=vmem(2),
        out_specs=vmem(1)[0],
        scratch_shapes=[
            pltpu.VMEM((B_PAIRS, Q_LOCAL, 8, LANE), BF16),
            pltpu.VMEM((8, 8, LANE), BF16),
            pltpu.VMEM((2, T_TILES, 8, LANE), BF16),
            pltpu.VMEM((8, 8, 8, LANE), BF16),
            pltpu.VMEM((64, 8, LANE), BF16),
            pltpu.VMEM((PARTS, 2, 8, 2, Q_LOCAL, 8, LANE), BF16),
            pltpu.VMEM((4, 4, 2, 8, Q_LOCAL, 8, LANE), BF16),
            pltpu.VMEM((LEFT_ROWS, 4, 4, 2, 8, LANE), BF16),
            pltpu.VMEM((2, 4, 2, 4, T_TILES, 8, LANE), BF16),
            pltpu.VMEM((deepest, KDIM), BF16),
            pltpu.VMEM((8, deepest, LANE), BF16),
            pltpu.VMEM((2 * NVP, deepest + 96), BF16),
            pltpu.VMEM((2 * NVP, KDIM), F32),
            pltpu.VMEM((2, KDIM, NVP), BF16),
            pltpu.VMEM((4, BLOCKS, GROUPS, 8, LANE), BF16),
            dma((PARTS,)), dma((PARTS,)), dma((PARTS,)), dma((PARTS,)),
            dma((6,)), dma((6,)), dma((4,)), dma((4,)), dma((2,)), dma((PARTS,)), dma,
            dma, dma,
        ],
        compiler_params=pltpu.CompilerParams(
            has_side_effects=True, vmem_limit_bytes=42 * MIB, collective_id=5
        ),
        name="ladder",
    )(factors, t_local)


def finish(blocks):
    turned = pl.pallas_call(
        finish_kernel,
        out_shape=shape(BLOCK, BLOCK, ROWS_X),
        in_specs=vmem(1),
        out_specs=vmem(1)[0],
        scratch_shapes=[pltpu.VMEM((ACTIVE, LANE, ROWS_P), F32)],
        compiler_params=pltpu.CompilerParams(vmem_limit_bytes=40 * MIB),
        name="finish",
    )(blocks)
    return turned.transpose(2, 0, 1)


def on_device(factors, amplitudes):
    return finish(ladder(factors, amplitudes))


def solution(mesh):
    in_specs = (P(("row", "col", "depth"), None, None), P("row", None, "depth"))
    out_specs = P("row", "depth", "col")
    return jax.shard_map(
        on_device, mesh=mesh, in_specs=in_specs, out_specs=out_specs, check_vma=False
    )
```

```python
import jax
import jax.numpy as jnp
from jax import lax
from jax.experimental import pallas as pl
from jax.experimental.pallas import tpu as pltpu
from jax.sharding import PartitionSpec as P

NV = 480
BLOCKS = 8
BLOCK = 60
PAD = 64
NVP = BLOCKS * PAD
LANE = 128
TILES = NVP // LANE
Q_LOCAL = 5
DEVICES = 256
NAUX = Q_LOCAL * DEVICES
CW = 3
ROWS_X = 132
GROUPS = 17
ROWS_P = GROUPS * 8
FOLD = 72
T_TILES = (GROUPS + FOLD // 8) // 2
B_PAIRS = 240
SLOTS = 15
ACTIVE = 2 * SLOTS
ORDER = ((2, 0), (2, 1), (1, 0), (1, 1), (3, 0), (3, 1), (0, 1), "beside", "own")
PARTS = len(ORDER)
GROUPED = (range(0, 5), range(5, 7), range(7, 9))
KDIM = CW * NVP
LEFT_ROWS = Q_LOCAL * CW * TILES
BF16 = jnp.bfloat16
F32 = jnp.float32
MIB = 1 << 20


def ones_where(mask):
    return jnp.where(mask, 1.0, 0.0).astype(BF16)


def iotas(rows, columns):
    shape = (rows, columns)
    return lax.broadcasted_iota(jnp.int32, shape, 0), lax.broadcasted_iota(jnp.int32, shape, 1)


def dot(left, right):
    return jnp.dot(left, right, preferred_element_type=F32)


def dot_nt(left, right):
    return lax.dot_general(left, right, (((1,), (1,)), ((), ())), preferred_element_type=F32)


def spread_matrix():
    row, column = iotas(NV, NVP)
    within = column & (PAD - 1)
    return ones_where((row == (column >> 6) * BLOCK + within) & (within < BLOCK))


def prepare(f_ref, t_ref, send_ref, left_ref, t_out_ref):
    spread = spread_matrix()
    out_row, in_row = iotas(LANE, LANE)
    gather_rows = ones_where(
        in_row == (out_row & 3) * 32 + (out_row >> 3) * 2 + ((out_row >> 2) & 1)
    )
    row, column = iotas(16, NV)
    pick = ones_where((row == column) & (row < CW))
    left_tiles = []
    for q in range(Q_LOCAL):
        wide = dot(f_ref[q], spread).astype(BF16)
        for chunk in range(NV // 32):
            rows = wide[32 * chunk : 32 * chunk + 32]
            stacked = jnp.concatenate(
                [rows[:, LANE * t : LANE * (t + 1)] for t in range(TILES)], axis=0
            )
            moved = dot(gather_rows, stacked).reshape(16, 8, LANE)
            send_ref[16 * chunk : 16 * chunk + 16, q] = moved.astype(BF16)
        picked = dot(dot_nt(pick, f_ref[q]).astype(BF16), spread).astype(BF16)
        left_tiles += [picked[:, LANE * t : LANE * (t + 1)] for t in range(TILES)]
    out_row, in_row = iotas(64, 64 * Q_LOCAL)
    place = ones_where(
        (out_row == (in_row >> 6) * 12 + (in_row & 15) * 4 + ((in_row >> 4) & 3))
        & ((in_row & 15) < CW)
    )
    left_ref[...] = dot(place, jnp.concatenate(left_tiles, axis=0)).reshape(8, 8, LANE).astype(BF16)
    row, column = iotas(BLOCK, LANE)
    low = ones_where(row == column)
    high = ones_where(row + PAD == column)
    both = (dot(t_ref[0], low) + dot(t_ref[1], high)).reshape(GROUPS, 8, LANE).astype(BF16)
    folded = dot(t_ref[2], low)[0:FOLD] + dot(t_ref[2], high)[ROWS_P - FOLD : ROWS_P]
    t_out_ref[0] = both[0:T_TILES]
    t_out_ref[1, 0 : GROUPS - T_TILES] = both[T_TILES:GROUPS]
    t_out_ref[1, GROUPS - T_TILES : T_TILES] = folded.reshape(FOLD // 8, 8, LANE).astype(BF16)


def place_of(row, col, depth):
    return row, depth // 2, (depth % 2) * 4 + col // 2, col % 2


def slot_of(x, y):
    return (y - x + 4) % 4 * 4 + x


def mesh_id(x, y, z, core):
    return {"row": x, "col": (z % 4) * 2 + core, "depth": y * 2 + z // 4}


def wait_bytes(ref, sem):
    pltpu.make_async_copy(ref, ref, sem).wait()


def ladder_kernel(
    f_ref, t_local, out_ref,
    send_ref, left_in, t_in, staged, bundle, relay, right_ref, left_ref, t_ref,
    left_rows, right_n, right_t, total, mid, blocks,
    z_send, z_recv, xy_send, xy_recv, l_send, l_recv, t_send, t_recv, own_sem, z_own, xy_own,
    out_send, out_recv,
):
    x, y, z, core = place_of(lax.axis_index("row"), lax.axis_index("col"), lax.axis_index("depth"))
    z_hi = z // 4
    active = slot_of(x, y) < SLOTS
    barrier = pltpu.get_barrier_semaphore()

    def greet(x, y, z, core):
        pl.semaphore_signal(
            barrier, inc=1, device_id=mesh_id(x, y, z, core), device_id_type=pl.DeviceIdType.MESH
        )

    @pl.loop(1, 16)
    def _(step):
        greet(x, y, (z + step) % 8, (core + step // 8) % 2)
        greet((x + step // 4) % 4, (y + step) % 4, z, core)
        greet((x + step // 4) % 4, (y + step) % 4, (z + 2) % 8, core)
        greet((x + step // 4) % 4, (y + step) % 4, (z + 6) % 8, core)

    prepare(f_ref, t_local, send_ref, left_in, t_in)
    pl.semaphore_wait(barrier, 60)
    half = LEFT_ROWS // 2

    def remote(src, dst, send, recv, to):
        return pltpu.make_async_remote_copy(
            src_ref=src, dst_ref=dst, send_sem=send, recv_sem=recv,
            device_id=mesh_id(*to), device_id_type=pl.DeviceIdType.MESH,
        )

    own_left = pltpu.make_async_copy(left_in, staged.at[z], own_sem.at[0])
    own_left.start()
    own_t = pltpu.make_async_copy(t_in.at[core], t_ref.at[core, y, z_hi, x], own_sem.at[1])
    own_t.start()
    remote(
        t_in.at[core], t_ref.at[core, y, z_hi, x], t_send.at[0], t_recv.at[0], (x, y, 7 - z, core)
    ).start()

    @pl.loop(1, 8)
    def _(step):
        remote(
            left_in, staged.at[z], l_send.at[0], l_recv.at[0], (x, y, (z + step) % 8, core)
        ).start()

    def width(part):
        return 1 if isinstance(ORDER[part], str) else 2

    def first_slot(part):
        if ORDER[part] == "own":
            return slot_of(x, y)
        if ORDER[part] == "beside":
            return slot_of(x, y) + 1 - 2 * (x % 2)
        diagonal, other = ORDER[part]
        return (y - x + diagonal + 4) % 4 * 4 + 2 * ((x // 2 + other) % 2)

    def by_count(part, act):
        short = first_slot(part) + width(part) > SLOTS
        if width(part) > 1:

            @pl.when(short)
            def _():
                act(width(part) - 1)

        @pl.when(jnp.logical_not(short))
        def _():
            act(width(part))

    def pair_at(to_z, to_core):
        return ACTIVE * (((to_z + 2) % 4) * 2 + to_core) + SLOTS * (to_z // 4)

    def send_along_z(part):
        first = first_slot(part)

        def send(count):
            @pl.loop(1, 16)
            def _(step):
                to_z, to_core = (z + step) % 8, (core + step // 8) % 2
                remote(
                    send_ref.at[pl.ds(pair_at(to_z, to_core) + first, count)],
                    relay.at[part, core, z, 0:count],
                    z_send.at[part], z_recv.at[part], (x, y, to_z, to_core),
                ).start()

            pltpu.make_async_copy(
                send_ref.at[pl.ds(pair_at(z, core) + first, count)],
                relay.at[part, core, z, 0:count],
                z_own.at[part],
            ).start()

        by_count(part, send)

    def pass_on(part):
        by_count(part, lambda count: wait_bytes(send_ref.at[0 : 15 * count], z_recv.at[part]))
        by_count(part, lambda count: wait_bytes(send_ref.at[0:count], z_own.at[part]))

        if ORDER[part] == "own":

            @pl.when(active)
            def _():
                pltpu.make_async_copy(
                    relay.at[part, :, :, 0], right_ref.at[x, y], xy_own
                ).start()

            return

        @pl.loop(0, width(part))
        def _(i):
            slot = first_slot(part) + i
            to_x = slot % 4

            @pl.when(slot < SLOTS)
            def _():
                remote(
                    relay.at[part, :, :, i], right_ref.at[x, y], xy_send.at[part],
                    xy_recv.at[part], (to_x, (to_x + slot // 4) % 4, z, core),
                ).start()

    send_along_z(0)
    send_along_z(1)

    own_left.wait()
    wait_bytes(staged.at[0:7], l_recv.at[0])
    out_row, in_row = iotas(64, 64)
    sort_rows = ones_where(in_row == ((out_row & 7) << 3) + (out_row >> 3))
    wide = jnp.concatenate(
        [staged[:, g].astype(F32).reshape(64, LANE) for g in range(8)], axis=1
    ).astype(BF16)
    wide = dot(sort_rows, wide)
    for g in range(8):
        block = wide[:, LANE * g : LANE * g + LANE].reshape(8, 8, LANE).astype(BF16)
        bundle[8 * g : 8 * g + 8] = block
    own_bundle = pltpu.make_async_copy(
        bundle.at[0:LEFT_ROWS], left_ref.at[:, x, y, core], own_sem.at[0]
    )
    own_bundle.start()
    own_t.wait()
    wait_bytes(t_ref.at[0, 0, 0, 0], t_recv.at[0])

    @pl.loop(1, 4)
    def _(step):
        remote(
            bundle.at[0:half], left_ref.at[0:half, x, y, core], l_send.at[1], l_recv.at[1],
            (x, (y + step) % 4, z, core),
        ).start()
        remote(
            bundle.at[half:LEFT_ROWS], left_ref.at[half:LEFT_ROWS, x, y, core],
            l_send.at[2], l_recv.at[2], ((x + step) % 4, y, z, core),
        ).start()
        block = t_ref.at[core, y, :, x]
        to = ((x + step * core) % 4, (y + step * (1 - core)) % 4, z, core)
        remote(block, block, t_send.at[1], t_recv.at[1], to).start()

    send_along_z(2)
    pass_on(0)
    send_along_z(3)

    own_bundle.wait()
    three_bundles = left_ref.at[0:half, 0, 0:3, 0]
    three_rings = left_ref.at[0:half, 0:3, :, 0]
    wait_bytes(three_bundles, l_recv.at[1])
    wait_bytes(three_bundles, l_recv.at[2])
    wait_bytes(t_ref.at[0, 0, :, 0:3], t_recv.at[1])

    @pl.loop(1, 4)
    def _(step):
        block = left_ref.at[0:half, x, :, core]
        remote(block, block, l_send.at[3], l_recv.at[3], ((x + step) % 4, y, z, core)).start()
        block = left_ref.at[half:LEFT_ROWS, :, y, core]
        remote(block, block, l_send.at[4], l_recv.at[4], (x, (y + step) % 4, z, core)).start()

        @pl.when(core == 0)
        def _():
            block = t_ref.at[0, :, :, x]
            remote(block, block, t_send.at[2], t_recv.at[2], ((x + step) % 4, y, z, core)).start()

        @pl.when(core == 1)
        def _():
            block = t_ref.at[1, y]
            remote(block, block, t_send.at[2], t_recv.at[2], (x, (y + step) % 4, z, core)).start()

    send_along_z(4)
    pass_on(1)
    send_along_z(5)
    pass_on(2)
    send_along_z(6)
    pass_on(3)
    send_along_z(7)
    send_along_z(8)

    wait_bytes(three_rings, l_recv.at[3])
    wait_bytes(three_rings, l_recv.at[4])
    sibling = (x, y, z, 1 - core)
    block = left_ref.at[:, :, :, core]
    swap_left = remote(block, block, l_send.at[5], l_recv.at[5], sibling)
    swap_left.start()
    wait_bytes(t_ref.at[0, 0:3], t_recv.at[2])
    block = t_ref.at[core]
    swap_t = remote(block, block, t_send.at[3], t_recv.at[3], sibling)
    swap_t.start()

    def columns(count):
        return right_ref.at[0, 0:count]

    out_row, in_row = iotas(256, 256)
    sort_rows = ones_where(in_row == ((out_row & 31) << 3) + (out_row >> 5))
    row, column = iotas(LANE, LANE)
    identity = ones_where(row == column)

    def sources(part):
        diagonal, other = (0, 0) if isinstance(ORDER[part], str) else ORDER[part]
        diagonal = (y - x - diagonal + 8) % 4
        from_x = 2 * ((x // 2 + other) % 2)
        return [(from_x + i, (from_x + i + diagonal) % 4) for i in range(2)]

    def pairs_of(group):
        return [part for part in GROUPED[group] if ORDER[part] != "own"]

    def sort_group(group):
        pairs = pairs_of(group)
        for chunk, part in enumerate(pairs):
            froms = sources(part)
            for q in range(Q_LOCAL):
                base = 32 * (Q_LOCAL * chunk + q)
                block = jnp.concatenate(
                    [
                        right_ref[from_x, from_y, :, :, q].astype(F32).reshape(LANE, LANE)
                        for from_x, from_y in froms
                    ],
                    axis=0,
                )
                moved = dot(sort_rows, block.astype(BF16)).astype(BF16)
                for r in range(8):
                    right_n[r, base : base + 32, :] = moved[32 * r : 32 * r + 32]
        depth = 32 * Q_LOCAL * len(pairs)
        for r in range(8):
            right_t[LANE * r : LANE * r + LANE, 0:depth] = dot_nt(
                identity, right_n[r, 0:depth, :]
            ).astype(BF16)

    def gather_left(group):
        for chunk, part in enumerate(pairs_of(group)):
            for i, (from_x, from_y) in enumerate(sources(part)):
                for r in range(LEFT_ROWS):
                    q, tile = divmod(r, CW * TILES)
                    base = 32 * (Q_LOCAL * chunk + q) + 16 * i
                    left_rows[base : base + 16, LANE * tile : LANE * tile + LANE] = left_ref[
                        r, from_x, from_y
                    ].reshape(16, LANE)

    def multiply(group):
        depth = 32 * Q_LOCAL * len(pairs_of(group))
        for m in range(4):
            which, half_of_d = divmod(m, 2)
            for c in range(CW):
                rows, lanes = slice(256 * m, 256 * m + 256), slice(NVP * c, NVP * c + NVP)
                rebuilt = dot(right_t[rows, 0:depth], left_rows[0:depth, lanes])
                if group > 0:
                    rebuilt += total[rows, lanes]
                if group < len(GROUPED) - 1:
                    total[rows, lanes] = rebuilt
                    continue
                rebuilt = rebuilt.astype(BF16)
                if c < 2:
                    for k in range(4):
                        base = (4 * half_of_d + k) * LANE + PAD * c
                        mid[which, base : base + PAD, :] = rebuilt[PAD * k : PAD * k + PAD]
                else:
                    base = 2 * NVP + 256 * half_of_d
                    mid[which, base : base + 256, :] = rebuilt

    def arrived(parts):
        for part in parts:
            if ORDER[part] == "own":
                wait_bytes(columns(1), xy_own)
            else:
                wait_bytes(columns(width(part)), xy_recv.at[part])

    pass_on(4)
    pass_on(5)

    @pl.when(active)
    def _():
        arrived(GROUPED[0])
        sort_group(0)

    pass_on(6)
    swap_left.wait_recv()

    @pl.when(active)
    def _():
        gather_left(0)
        multiply(0)

    pass_on(7)

    @pl.when(active)
    def _():
        arrived(GROUPED[1])
        sort_group(1)
        gather_left(1)
        multiply(1)

    pass_on(8)
    swap_t.wait_recv()
    slot = SLOTS * z_hi + slot_of(x, y)

    @pl.when(active)
    def _():
        gather_left(2)
        arrived(GROUPED[2])
        sort_group(2)
        multiply(2)
        first_half = lax.broadcasted_iota(jnp.int32, (ROWS_P, LANE), 1) < PAD

        @pl.loop(0, 4)
        def _(turn):
            to_x = (x + 2 + turn - turn // 2 * (2 * turn - 1)) % 4

            def tiles_of(half, k, first, last):
                return t_ref[half, k // 2, k % 2, to_x, first:last].astype(F32)

            def side_by_side(k):
                rest = GROUPS - T_TILES
                whole = [tiles_of(0, k, 0, T_TILES), tiles_of(1, k, 0, rest)]
                return jnp.concatenate(whole, axis=0).reshape(ROWS_P, LANE)

            def unfolded(k):
                one, two = (
                    tiles_of(1, k + i, GROUPS - T_TILES, T_TILES).reshape(FOLD, LANE)
                    for i in range(2)
                )
                begin = first_half[0:FOLD]
                top = jnp.where(begin, one, pltpu.roll(two, PAD, 1))
                bottom = jnp.where(begin, pltpu.roll(one, PAD, 1), two)
                return jnp.concatenate([top, bottom[2 * FOLD - ROWS_P : FOLD]], axis=0)

            tiles = [side_by_side(k) for k in range(BLOCKS)]
            tiles += [unfolded(2 * k) for k in range(4)]
            t_rows = jnp.concatenate(tiles, axis=1).astype(BF16)
            totals = [dot(t_rows, mid[which]) for which in range(2)]
            for k in range(4):
                lanes = slice(LANE * k, LANE * k + LANE)
                one, two = totals[0][:, lanes], totals[1][:, lanes]
                even = jnp.where(first_half, one, pltpu.roll(two, PAD, 1))
                odd = jnp.where(first_half, pltpu.roll(one, PAD, 1), two)
                blocks[to_x, 2 * k] = even.reshape(GROUPS, 8, LANE).astype(BF16)
                blocks[to_x, 2 * k + 1] = odd.reshape(GROUPS, 8, LANE).astype(BF16)

            @pl.loop(0, 8)
            def _(step):
                to_y, to_z = (y + step // 2) % 4, (z + 2 + 4 * (step % 2)) % 8
                pltpu.make_async_remote_copy(
                    src_ref=blocks.at[to_x, to_y * 2 + to_z // 4],
                    dst_ref=out_ref.at[slot],
                    send_sem=out_send,
                    recv_sem=out_recv,
                    device_id=mesh_id(to_x, to_y, to_z, core),
                    device_id_type=pl.DeviceIdType.MESH,
                ).start()

    wait_bytes(out_ref.at[0:ACTIVE], out_recv)

    @pl.when(active)
    def _():
        wait_bytes(blocks, out_send)

    swap_left.wait_send()
    swap_t.wait_send()
    wait_bytes(staged.at[0:7], l_send.at[0])
    wait_bytes(three_bundles, l_send.at[1])
    wait_bytes(three_bundles, l_send.at[2])
    wait_bytes(three_rings, l_send.at[3])
    wait_bytes(three_rings, l_send.at[4])
    wait_bytes(t_ref.at[0, 0, 0, 0], t_send.at[0])
    wait_bytes(t_ref.at[0, 0, :, 0:3], t_send.at[1])
    wait_bytes(t_ref.at[0, 0:3], t_send.at[2])

    for part in range(PARTS):
        by_count(part, lambda count: wait_bytes(send_ref.at[0 : 15 * count], z_send.at[part]))

    for part in range(PARTS - 1):
        by_count(part, lambda count: wait_bytes(columns(count), xy_send.at[part]))

def finish_kernel(in_ref, out_ref, turned):
    row, column = iotas(LANE, LANE)
    identity = ones_where(row == column)
    for group in range(ACTIVE):
        block = in_ref[group].astype(F32).reshape(ROWS_P, LANE).astype(BF16)
        turned[group] = dot_nt(identity, block)
    rows = 2 * ACTIVE * 8
    out_row, in_row = iotas(512, rows)
    sort_rows = ones_where(in_row == ((out_row & 63) << 3) + (out_row >> 6))
    for chunk in range(8):
        parts = []
        for group in range(ACTIVE):
            for which in range(2):
                base = PAD * which + 8 * chunk
                parts.append(turned[group, base : base + 8, :])
        moved = dot(sort_rows, jnp.concatenate(parts, axis=0).astype(BF16)).astype(BF16)
        for a in range(8 if chunk < 7 else 4):
            out_ref[8 * chunk + a] = moved[64 * a : 64 * a + 64][0:BLOCK, 0:ROWS_X]


def vmem(count):
    return [pl.BlockSpec(memory_space=pltpu.VMEM)] * count


def anywhere(count):
    return [pl.BlockSpec(memory_space=pl.ANY)] * count


def shape(*sizes):
    return jax.ShapeDtypeStruct(sizes, BF16)


def ladder(factors, amplitudes):
    dma = pltpu.SemaphoreType.DMA
    t_local = jnp.pad(amplitudes.transpose(1, 0, 2), ((0, 0), (0, ROWS_P - ROWS_X), (0, 0)))
    deepest = 32 * Q_LOCAL * 5
    return pl.pallas_call(
        ladder_kernel,
        out_shape=shape(32, GROUPS, 8, LANE),
        in_specs=vmem(2),
        out_specs=vmem(1)[0],
        scratch_shapes=[
            pltpu.VMEM((B_PAIRS, Q_LOCAL, 8, LANE), BF16),
            pltpu.VMEM((8, 8, LANE), BF16),
            pltpu.VMEM((2, T_TILES, 8, LANE), BF16),
            pltpu.VMEM((8, 8, 8, LANE), BF16),
            pltpu.VMEM((64, 8, LANE), BF16),
            pltpu.VMEM((PARTS, 2, 8, 2, Q_LOCAL, 8, LANE), BF16),
            pltpu.VMEM((4, 4, 2, 8, Q_LOCAL, 8, LANE), BF16),
            pltpu.VMEM((LEFT_ROWS, 4, 4, 2, 8, LANE), BF16),
            pltpu.VMEM((2, 4, 2, 4, T_TILES, 8, LANE), BF16),
            pltpu.VMEM((deepest, KDIM), BF16),
            pltpu.VMEM((8, deepest, LANE), BF16),
            pltpu.VMEM((2 * NVP, deepest + 96), BF16),
            pltpu.VMEM((2 * NVP, KDIM), F32),
            pltpu.VMEM((2, KDIM, NVP), BF16),
            pltpu.VMEM((4, BLOCKS, GROUPS, 8, LANE), BF16),
            dma((PARTS,)), dma((PARTS,)), dma((PARTS,)), dma((PARTS,)),
            dma((6,)), dma((6,)), dma((4,)), dma((4,)), dma((2,)), dma((PARTS,)), dma,
            dma, dma,
        ],
        compiler_params=pltpu.CompilerParams(
            has_side_effects=True, vmem_limit_bytes=42 * MIB, collective_id=5
        ),
        name="ladder",
    )(factors, t_local)


def finish(blocks):
    turned = pl.pallas_call(
        finish_kernel,
        out_shape=shape(BLOCK, BLOCK, ROWS_X),
        in_specs=vmem(1),
        out_specs=vmem(1)[0],
        scratch_shapes=[pltpu.VMEM((ACTIVE, LANE, ROWS_P), F32)],
        compiler_params=pltpu.CompilerParams(vmem_limit_bytes=40 * MIB),
        name="finish",
    )(blocks)
    return turned.transpose(2, 0, 1)


def on_device(factors, amplitudes):
    return finish(ladder(factors, amplitudes))


def solution(mesh):
    in_specs = (P(("row", "col", "depth"), None, None), P("row", None, "depth"))
    out_specs = P("row", "depth", "col")
    return jax.shard_map(
        on_device, mesh=mesh, in_specs=in_specs, out_specs=out_specs, check_vma=False
    )
```
